32 devices in a mesh: rows: 8 (over z, y), rhs: 4 (over x, core).
Axes of the slice: x: 2, y: 2, z: 4, core: 2. Of those that a mesh axis runs over, the one named last changes fastest.
Arguments:
- right_side: bfloat16 [64, 512, 256], P('rows', 'rhs'), may hold values from -6 to 6
- off_blocks: bfloat16 [64, 8, 256, 256], P('rows', None, 'rhs'), may hold values from -0.125 to 0.125
- diag_inverse: bfloat16 [64, 256, 256], P('rows', 'rhs'), may hold values from -0.375 to 0.375
- block_level: int32 [64], P('rows'), may hold values from 0 to 3, as said below
- block_columns: int32 [64, 8], P('rows'), may hold values from 0 to 63, as said below
Outputs:
- solved: bfloat16 [64, 512, 256], P('rows', 'rhs')
The draws below stay inside these ranges and needn't reach their ends.
Inputs may be any that keep to these rules, and one draw needn't show every extreme that they name: `block_level`: among the 8 block rows of one index of rows every level occurs, none more than 4 times, and one level exactly 4 times. `block_columns`: block row i lies on index i // 8 of rows; each of its 8 block columns is a block row on the same index or one of the 3 indices below it (none below 0), of lower level when block row i has level 1 or more. Columns of one block row may repeat.
All inputs are finite; a program needn't handle non-finite values.
Results may differ from the reference program's by a relative error of at most 0.0075.
Values may be sent and summed in bfloat16 or wider, within the bound.
A program may use at most 128 MiB of HBM per device.

```python
import jax
import jax.numpy as jnp
from jax import lax

BS = 256
K = 8
LEVELS = 4
REACH = 4
BR_DEV = 8
CAP = 4
NB = 64
RHS = 512


def level_table(key):
    groups = NB // BR_DEV
    heavy_key = jax.random.fold_in(key, 101)
    rest_key = jax.random.fold_in(key, 102)
    order_key = jax.random.fold_in(key, 103)
    heavy = jax.random.randint(heavy_key, (groups,), 0, LEVELS)
    each_once = (heavy[:, None] + 1 + jnp.arange(LEVELS - 1, dtype=jnp.int32)[None, :]) % LEVELS
    extra = BR_DEV - CAP - (LEVELS - 1)
    others = jax.random.randint(rest_key, (groups, extra), 0, LEVELS - 1)
    others = (heavy[:, None] + 1 + others) % LEVELS
    slots = jnp.concatenate([jnp.broadcast_to(heavy[:, None], (groups, CAP)), each_once, others], axis=1)
    scores = jax.random.randint(order_key, (groups, BR_DEV), 0, 2 ** 20) * BR_DEV
    scores = scores + jnp.arange(BR_DEV, dtype=jnp.int32)[None, :]
    ranking = jnp.argsort(scores, axis=1)
    return jnp.take_along_axis(slots, ranking, axis=1).reshape(NB).astype(jnp.int32)


def draw_block_level(key, part):
    return level_table(key)


def draw_block_columns(key, part):
    levels = level_table(key)
    key = jax.random.fold_in(key, 7)
    column_ids = jnp.arange(NB, dtype=jnp.int32)
    owner = column_ids // BR_DEV
    near = (owner[None, :] <= owner[:, None]) & (owner[None, :] > owner[:, None] - REACH)
    lower = (levels[None, :] < levels[:, None]) | (levels[:, None] == 0)
    allowed = near & lower
    scores = jax.random.randint(key, (NB, K, NB), 0, 2 ** 16) * NB + column_ids[None, None, :]
    scores = jnp.where(allowed[:, None, :], scores, -1)
    chosen = jnp.argmax(scores, axis=2)
    return chosen.astype(jnp.int32)


def shard_levels(rng, extent, split, low, largest):
    level, own = 1.0, jax.random.fold_in(rng, 6)
    for axis_at, parts in split:
        heights = jnp.exp(jax.random.uniform(jax.random.fold_in(own, axis_at), (parts,), jnp.float32, low / len(split), largest / len(split)))
        level = level * jnp.repeat(heights, extent[axis_at] // parts).reshape([-1 if axis == axis_at else 1 for axis in range(len(extent))])
    return level


def centred(own_key, shape, deviation, most, pieces=(), held_as=jnp.bfloat16):
    array = jax.random.normal(own_key, shape, jnp.float32) * deviation
    if len(pieces) > 0:
        array = shard_levels(own_key, shape, pieces, -0.22, 0.18) * array
    return jnp.clip(array, min=-most, max=most).astype(held_as)


def setup_inputs(seed: int = 0) -> dict:
    seeds = jax.random.split(jax.random.key(seed), 6)
    right_side = centred(seeds[0], (NB, RHS, BS), 1.0, 6.0, ((0, 8), (1, 4)))
    off_blocks = centred(seeds[1], (NB, K, BS, BS), (BS * K) ** -0.5, 0.125, ((0, 8), (2, 4)))
    diag_inverse = centred(seeds[2], (NB, BS, BS), BS ** -0.5, 0.375, ((0, 8), (1, 4)))
    block_level = draw_block_level(jax.random.fold_in(seeds[5], 71), 0)
    block_columns = draw_block_columns(jax.random.fold_in(seeds[5], 71), 0)
    return {"right_side": right_side, "off_blocks": off_blocks, "diag_inverse": diag_inverse, "block_level": block_level, "block_columns": block_columns}


def reference(right_side, off_blocks, diag_inverse, block_level, block_columns):
    solved = jnp.zeros(right_side.shape, jnp.bfloat16)
    for level_now in range(LEVELS):
        def one_row(items, current=solved):
            blocks, inverse, rhs_row, cols_row = items
            picked = jnp.take(current, cols_row.astype(jnp.int32), axis=0).astype(jnp.float32)
            contribution = jnp.einsum("krb,kab->ra", picked, blocks.astype(jnp.float32))
            residue = (rhs_row.astype(jnp.float32) - contribution).astype(jnp.bfloat16)
            residue = lax.optimization_barrier(residue)
            updated = jnp.einsum("rb,ab->ra", residue.astype(jnp.float32), inverse.astype(jnp.float32))
            return updated.astype(jnp.bfloat16)

        updated = lax.map(one_row, (off_blocks, diag_inverse, right_side, block_columns))
        solved = jnp.where((block_level == level_now)[:, None, None], updated, solved)
        solved = lax.optimization_barrier(solved)
    return solved
```

```python
import functools

import jax
import jax.numpy as jnp
from jax import lax
from jax.experimental import pallas as pl
from jax.experimental.pallas import tpu as pltpu
from jax.sharding import PartitionSpec as P

REACH = 4
BELOW = REACH - 1
MESH = pl.DeviceIdType.MESH
FIRST = (0, 1, 2, 4)
LAST = (3, 5, 6, 7)
AHEAD = 3


def nt(a, b):
    return lax.dot_general(a, b, (((1,), (1,)), ((), ())), preferred_element_type=jnp.float32)


def kernel(
    n, level_ref, cols_ref, lvl_ref, right_ref, off_ref, diag_ref, out_ref,
    fac, inv, win, land0, land1, land2, sol0, sol1, sol2, fin, lvl_in, lvl_s, rank, perm, lev,
    lvl_send, lvl_recv, lvl_sem, x_send, x_recv, c_send, c_recv, f_send, f_recv,
    w0_send, w0_recv, w1_send, w1_recv, w2_send, w2_recv,
):
    rows, kk, part, bs = off_ref.shape
    me, mine = lax.axis_index("rows"), lax.axis_index("rhs")
    core = mine + 1 - 2 * lax.rem(mine, 2)
    across = lax.rem(mine + 2, 4)

    lvl_in[...] = jnp.zeros_like(lvl_in)
    barrier = pltpu.get_barrier_semaphore()
    for other in (core, across):
        pl.semaphore_signal(barrier, inc=1, device_id=(me, other), device_id_type=MESH)
    for d in range(1, REACH):
        @pl.when(me + d < n)
        def _():
            pl.semaphore_signal(barrier, inc=1, device_id=(me + d, mine), device_id_type=MESH)

        @pl.when(me >= d)
        def _():
            pl.semaphore_signal(barrier, inc=1, device_id=(me - d, mine), device_id_type=MESH)

    own = [level_ref[r] for r in range(rows)]

    def ranked(levels, base):
        out = []
        for r in range(rows):
            before = jnp.int32(0)
            for q in range(rows):
                if q < r:
                    before += (levels[q] <= levels[r]).astype(jnp.int32)
                elif q > r:
                    before += (levels[q] < levels[r]).astype(jnp.int32)
            rank[base + r] = before
            out.append(before)
        return out

    own_rank = ranked(own, BELOW * rows)
    where = []
    for p in range(rows):
        at = jnp.int32(0)
        for r in range(rows):
            at += jnp.where(own_rank[r] == p, r, 0)
        perm[p] = at
        lev[p] = level_ref[at]
        where.append(at)

    def span(who):
        return pl.ds(pl.multiple_of(who * part, part), part)

    def stage_diag(p):
        inv[p, span(mine), :] = diag_ref[where[p]]

    def stage_off(p):
        for k in range(kk):
            fac[p - 1, span(mine), k * bs:(k + 1) * bs] = off_ref[where[p], k]

    half = rows // 2
    items = [("d", 0)] + [("o", p) for p in range(1, half)] + [("d", 1)] + [("o", p) for p in range(half, rows)]

    def piece(item, who):
        kind, at = item
        if kind == "d":
            return inv.at[at * half:(at + 1) * half, span(who), :]
        return fac.at[at - 1, span(who), :]

    def send_x(i):
        return pltpu.make_async_remote_copy(
            piece(items[i], mine), piece(items[i], mine), x_send.at[i], x_recv.at[i],
            device_id=(me, across), device_id_type=MESH)

    def send_c(i):
        return pltpu.make_async_remote_copy(
            piece(items[i], mine), piece(items[i], mine), c_send.at[i], c_recv.at[i],
            device_id=(me, core), device_id_type=MESH)

    def send_f(i):
        return pltpu.make_async_remote_copy(
            piece(items[i], across), piece(items[i], across), f_send.at[i], f_recv.at[i],
            device_id=(me, core), device_id_type=MESH)

    def issue(i):
        if i < len(items):
            send_x(i).start()
            send_c(i).start()

    def arrive(i):
        send_x(i).wait_recv()
        send_f(i).start()
        send_x(i).wait_send()
        issue(i + AHEAD)
        send_c(i).wait_recv()
        send_f(i).wait_recv()

    for p in range(rows):
        stage_diag(p)
        if p > 0:
            stage_off(p)

    greeted = jnp.int32(2)
    for d in range(1, REACH):
        greeted += (me + d < n).astype(jnp.int32) + (me >= d).astype(jnp.int32)
    pl.semaphore_wait(barrier, greeted)

    for i in range(AHEAD):
        issue(i)

    def upward(src, dst, s, r, d):
        return pltpu.make_async_remote_copy(
            src, dst, s, r, device_id=(me + d, mine), device_id_type=MESH)

    def send_lvl(d):
        return upward(lvl_ref, lvl_in.at[BELOW - d], lvl_send.at[d - 1], lvl_recv.at[d - 1], d)

    def send_0(d):
        return upward(sol0, land0.at[BELOW - d], w0_send.at[d - 1], w0_recv.at[d - 1], d)

    def send_1(i, d):
        return upward(sol1.at[i], land1.at[BELOW - d, i], w1_send.at[i, d - 1], w1_recv.at[i, d - 1], d)

    def send_2(i, d):
        return upward(sol2.at[i], land2.at[BELOW - d, i], w2_send.at[i, d - 1], w2_recv.at[i, d - 1], d)

    def each_up(what):
        for d in range(1, REACH):
            @pl.when(me + d < n)
            def _():
                what(d)

    def each_down(what):
        for d in range(1, REACH):
            @pl.when(me >= d)
            def _():
                what(d)

    each_up(lambda d: send_lvl(d).start())

    arrive(0)
    for p in range(half):
        sol0[p] = nt(right_ref[where[p]], inv[p]).astype(jnp.bfloat16)
    each_up(lambda d: send_0(d).start())

    each_down(lambda d: send_lvl(d).wait_recv())
    fetch = pltpu.make_async_copy(lvl_in, lvl_s, lvl_sem)
    fetch.start()
    fetch.wait()
    for o in range(BELOW):
        ranked([lvl_s[o, r, 0] for r in range(rows)], o * rows)

    def picked(p):
        taken = []
        for k in range(kk):
            at = cols_ref[perm[p], k] - (me - BELOW) * rows
            at = jnp.clip(at, 0, REACH * rows - 1)
            taken.append(win[at - lax.rem(at, rows) + rank[at]])
        return jnp.concatenate(taken, axis=1)

    def solve(p):
        contribution = nt(picked(p), fac[p - 1])
        residue = (right_ref[perm[p]].astype(jnp.float32) - contribution).astype(jnp.bfloat16)
        return nt(residue, inv[p])

    def keep(p, level_now, updated, before):
        if before is None:
            return updated.astype(jnp.bfloat16)
        return jnp.where(lev[p] == level_now, updated, before.astype(jnp.float32)).astype(jnp.bfloat16)

    def fill(land, sol, first):
        count = sol.shape[0]
        for d in range(1, REACH):
            o = BELOW - d
            win[o * rows + first:o * rows + first + count] = land[o]
        win[BELOW * rows + first:BELOW * rows + first + count] = sol[...]

    each_down(lambda d: send_0(d).wait_recv())
    fill(land0, sol0, 0)

    at_item = {p: items.index(("o", p)) for p in range(1, rows)}
    for p in range(FIRST[1], LAST[1] + 1):
        if p == half:
            arrive(half)
        arrive(at_item[p])
        i = p - FIRST[1]
        sol1[i] = keep(p, 1, solve(p), sol0[p] if p <= LAST[0] else None)
        each_up(lambda d: send_1(i, d).start())
    count1 = LAST[1] - FIRST[1] + 1
    each_down(lambda d: [send_1(i, d).wait_recv() for i in range(count1)])
    fill(land1, sol1, FIRST[1])

    for p in range(FIRST[2], LAST[2] + 1):
        if p == LAST[2]:
            arrive(at_item[p])
        i = p - FIRST[2]
        sol2[i] = keep(p, 2, solve(p), sol1[p - FIRST[1]] if p <= LAST[1] else None)
        each_up(lambda d: send_2(i, d).start())
    count2 = LAST[2] - FIRST[2] + 1
    arrive(at_item[rows - 1])
    each_down(lambda d: [send_2(i, d).wait_recv() for i in range(count2)])
    fill(land2, sol2, FIRST[2])

    fin[0] = sol0[0]
    fin[1] = sol1[0]
    for p in range(FIRST[2], FIRST[3]):
        fin[p] = sol2[p - FIRST[2]]
    for p in range(FIRST[3], rows):
        fin[p] = keep(p, 3, solve(p), sol2[p - FIRST[2]] if p <= LAST[2] else None)
    for r in range(rows):
        out_ref[r] = fin[rank[BELOW * rows + r]]

    for i in range(len(items)):
        send_c(i).wait_send()
        send_f(i).wait_send()

    def drain(d):
        send_lvl(d).wait_send()
        send_0(d).wait_send()
        for i in range(count1):
            send_1(i, d).wait_send()
        for i in range(count2):
            send_2(i, d).wait_send()

    each_up(drain)


def per_device(n, right_side, off_blocks, diag_inverse, block_level, block_columns):
    rows, kk, part, bs = off_blocks.shape
    samples = right_side.shape[1]
    vmem = pl.BlockSpec(memory_space=pltpu.VMEM)
    smem = pl.BlockSpec(memory_space=pltpu.SMEM)
    tile = (samples, bs)
    counts = [b - a + 1 for a, b in zip(FIRST, LAST)]
    items = rows + 1
    dma = pltpu.SemaphoreType.DMA
    return pl.pallas_call(
        functools.partial(kernel, n),
        out_shape=jax.ShapeDtypeStruct(right_side.shape, jnp.bfloat16),
        in_specs=[smem, smem, vmem, vmem, vmem, vmem],
        out_specs=vmem,
        scratch_shapes=[
            pltpu.VMEM((rows - 1, 4 * part, kk * bs), jnp.bfloat16),
            pltpu.VMEM((rows, 4 * part, bs), jnp.bfloat16),
            pltpu.VMEM((REACH * rows,) + tile, jnp.bfloat16),
            pltpu.VMEM((BELOW, counts[0]) + tile, jnp.bfloat16),
            pltpu.VMEM((BELOW, counts[1]) + tile, jnp.bfloat16),
            pltpu.VMEM((BELOW, counts[2]) + tile, jnp.bfloat16),
            pltpu.VMEM((counts[0],) + tile, jnp.bfloat16),
            pltpu.VMEM((counts[1],) + tile, jnp.bfloat16),
            pltpu.VMEM((counts[2],) + tile, jnp.bfloat16),
            pltpu.VMEM((rows,) + tile, jnp.bfloat16),
            pltpu.VMEM((BELOW, rows, 128), jnp.int32),
            pltpu.SMEM((BELOW, rows, 128), jnp.int32),
            pltpu.SMEM((REACH * rows,), jnp.int32),
            pltpu.SMEM((rows,), jnp.int32),
            pltpu.SMEM((rows,), jnp.int32),
            dma((BELOW,)), dma((BELOW,)), dma,
            dma((items,)), dma((items,)), dma((items,)), dma((items,)), dma((items,)), dma((items,)),
            dma((BELOW,)), dma((BELOW,)),
            dma((counts[1], BELOW)), dma((counts[1], BELOW)),
            dma((counts[2], BELOW)), dma((counts[2], BELOW)),
        ],
        compiler_params=pltpu.CompilerParams(
            collective_id=0, has_side_effects=True, vmem_limit_bytes=48 * 2 ** 20),
    )(
        block_level, block_columns,
        jnp.broadcast_to(block_level[:, None], (rows, 128)),
        right_side, off_blocks, diag_inverse,
    )


def solution(mesh):
    return jax.shard_map(
        functools.partial(per_device, mesh.shape["rows"]),
        mesh=mesh,
        in_specs=(
            P("rows", "rhs", None),
            P("rows", None, "rhs", None),
            P("rows", "rhs", None),
            P("rows"),
            P("rows", None),
        ),
        out_specs=P("rows", "rhs", None),
        check_vma=False,
    )
```

```python
import functools

import jax
import jax.numpy as jnp
from jax import lax
from jax.experimental import pallas as pl
from jax.experimental.pallas import tpu as pltpu
from jax.sharding import PartitionSpec as P

REACH = 4
BELOW = REACH - 1
MESH = pl.DeviceIdType.MESH
FIRST = (0, 1, 2, 4)
LAST = (3, 5, 6, 7)
AHEAD = 3


def nt(a, b):
    return lax.dot_general(a, b, (((1,), (1,)), ((), ())), preferred_element_type=jnp.float32)


def kernel(
    n, level_ref, cols_ref, lvl_ref, right_ref, off_ref, diag_ref, out_ref,
    fac, inv, win, land0, land1, land2, sol0, sol1, sol2, fin, lvl_in, lvl_s, rank, perm, lev,
    lvl_send, lvl_recv, lvl_sem, x_send, x_recv, c_send, c_recv, f_send, f_recv,
    w0_send, w0_recv, w1_send, w1_recv, w2_send, w2_recv,
):
    rows, kk, part, bs = off_ref.shape
    me, mine = lax.axis_index("rows"), lax.axis_index("rhs")
    core = mine + 1 - 2 * lax.rem(mine, 2)
    across = lax.rem(mine + 2, 4)

    lvl_in[...] = jnp.zeros_like(lvl_in)
    barrier = pltpu.get_barrier_semaphore()
    for other in (core, across):
        pl.semaphore_signal(barrier, inc=1, device_id=(me, other), device_id_type=MESH)
    for d in range(1, REACH):
        @pl.when(me + d < n)
        def _():
            pl.semaphore_signal(barrier, inc=1, device_id=(me + d, mine), device_id_type=MESH)

        @pl.when(me >= d)
        def _():
            pl.semaphore_signal(barrier, inc=1, device_id=(me - d, mine), device_id_type=MESH)

    own = [level_ref[r] for r in range(rows)]

    def ranked(levels, base):
        out = []
        for r in range(rows):
            before = jnp.int32(0)
            for q in range(rows):
                if q < r:
                    before += (levels[q] <= levels[r]).astype(jnp.int32)
                elif q > r:
                    before += (levels[q] < levels[r]).astype(jnp.int32)
            rank[base + r] = before
            out.append(before)
        return out

    own_rank = ranked(own, BELOW * rows)
    where = []
    for p in range(rows):
        at = jnp.int32(0)
        for r in range(rows):
            at += jnp.where(own_rank[r] == p, r, 0)
        perm[p] = at
        lev[p] = level_ref[at]
        where.append(at)

    def span(who):
        return pl.ds(pl.multiple_of(who * part, part), part)

    def stage_diag(p):
        inv[p, span(mine), :] = diag_ref[where[p]]

    def stage_off(p):
        for k in range(kk):
            fac[p - 1, span(mine), k * bs:(k + 1) * bs] = off_ref[where[p], k]

    half = rows // 2
    items = [("d", 0)] + [("o", p) for p in range(1, half)] + [("d", 1)] + [("o", p) for p in range(half, rows)]

    def piece(item, who):
        kind, at = item
        if kind == "d":
            return inv.at[at * half:(at + 1) * half, span(who), :]
        return fac.at[at - 1, span(who), :]

    def send_x(i):
        return pltpu.make_async_remote_copy(
            piece(items[i], mine), piece(items[i], mine), x_send.at[i], x_recv.at[i],
            device_id=(me, across), device_id_type=MESH)

    def send_c(i):
        return pltpu.make_async_remote_copy(
            piece(items[i], mine), piece(items[i], mine), c_send.at[i], c_recv.at[i],
            device_id=(me, core), device_id_type=MESH)

    def send_f(i):
        return pltpu.make_async_remote_copy(
            piece(items[i], across), piece(items[i], across), f_send.at[i], f_recv.at[i],
            device_id=(me, core), device_id_type=MESH)

    def issue(i):
        if i < len(items):
            send_x(i).start()
            send_c(i).start()

    def arrive(i):
        send_x(i).wait_recv()
        send_f(i).start()
        send_x(i).wait_send()
        issue(i + AHEAD)
        send_c(i).wait_recv()
        send_f(i).wait_recv()

    for p in range(rows):
        stage_diag(p)
        if p > 0:
            stage_off(p)

    greeted = jnp.int32(2)
    for d in range(1, REACH):
        greeted += (me + d < n).astype(jnp.int32) + (me >= d).astype(jnp.int32)
    pl.semaphore_wait(barrier, greeted)

    for i in range(AHEAD):
        issue(i)

    def send_lvl(d):
        return pltpu.make_async_remote_copy(
            lvl_ref, lvl_in.at[BELOW - d], lvl_send.at[d - 1], lvl_recv.at[d - 1],
            device_id=(me + d, mine), device_id_type=MESH)

    def each_up(what):
        for d in range(1, REACH):
            @pl.when(me + d < n)
            def _():
                what(d)

    def each_down(what):
        for d in range(1, REACH):
            @pl.when(me >= d)
            def _():
                what(d)

    even = lax.rem(me, 2) == 0
    odd = lax.rem(me, 2) == 1
    sols, lands = (sol0, sol1, sol2), (land0, land1, land2)
    hop_send, hop_recv = (w0_send, w1_send, w2_send), (w0_recv, w1_recv, w2_recv)
    OWN_UP, OWN_SIDE, PASS_SIDE, PASS_UP = range(4)

    def hop(v, i, way, to, d):
        src = sols[v].at[i]
        if way == PASS_SIDE:
            src = lands[v].at[BELOW - 2, i]
        if way == PASS_UP:
            src = lands[v].at[BELOW - 1, i]
        return pltpu.make_async_remote_copy(
            src, lands[v].at[BELOW - d, i], hop_send[v].at[i, way], hop_recv[v].at[i, d - 1],
            device_id=(to, mine), device_id_type=MESH)

    def landed(v, i, d):
        hop(v, i, OWN_UP, me, d).wait_recv()

    def own_hops(v, i, what):
        @pl.when(me + 2 < n)
        def _():
            what(hop(v, i, OWN_UP, me + 2, 2))

        @pl.when(even)
        def _():
            what(hop(v, i, OWN_SIDE, me + 1, 1))

    def side_hops(v, i, what):
        @pl.when(even & (me >= 2))
        def _():
            what(hop(v, i, PASS_SIDE, me + 1, 3))

        @pl.when(odd & (me >= 2))
        def _():
            what(hop(v, i, PASS_SIDE, me - 1, 1))

    def up_hops(v, i, what):
        @pl.when(even & (me >= 2) & (me + 2 < n))
        def _():
            what(hop(v, i, PASS_UP, me + 2, 3))

    def start(copy):
        copy.start()

    def first_leg(v, i):
        @pl.when(me >= 2)
        def _():
            landed(v, i, 2)
        side_hops(v, i, start)

    def second_leg(v, i):
        @pl.when(me >= 1)
        def _():
            landed(v, i, 1)
        up_hops(v, i, start)

    def third_leg(v, i):
        @pl.when(me >= 3)
        def _():
            landed(v, i, 3)

    def serve(v, i):
        count = sols[v].shape[0]
        for leg, late in ((first_leg, 1), (second_leg, 2), (third_leg, 3)):
            if 0 <= i - late < count:
                leg(v, i - late)

    def serve_rest(v):
        count = sols[v].shape[0]
        for i in range(count, count + 3):
            serve(v, i)

    each_up(lambda d: send_lvl(d).start())

    at_item = {p: items.index(("o", p)) for p in range(1, rows)}
    arrive(0)
    for p in range(half):
        sol0[p] = nt(right_ref[where[p]], inv[p]).astype(jnp.bfloat16)
        own_hops(0, p, start)

    each_down(lambda d: send_lvl(d).wait_recv())
    fetch = pltpu.make_async_copy(lvl_in, lvl_s, lvl_sem)
    fetch.start()
    fetch.wait()
    for o in range(BELOW):
        ranked([lvl_s[o, r, 0] for r in range(rows)], o * rows)

    def picked(p):
        taken = []
        for k in range(kk):
            at = cols_ref[perm[p], k] - (me - BELOW) * rows
            at = jnp.clip(at, 0, REACH * rows - 1)
            taken.append(win[at - lax.rem(at, rows) + rank[at]])
        return jnp.concatenate(taken, axis=1)

    def solve(p):
        contribution = nt(picked(p), fac[p - 1])
        residue = (right_ref[perm[p]].astype(jnp.float32) - contribution).astype(jnp.bfloat16)
        return nt(residue, inv[p])

    def keep(p, level_now, updated, before):
        if before is None:
            return updated.astype(jnp.bfloat16)
        return jnp.where(lev[p] == level_now, updated, before.astype(jnp.float32)).astype(jnp.bfloat16)

    def fill(land, sol, first):
        count = sol.shape[0]
        for d in range(1, REACH):
            o = BELOW - d
            win[o * rows + first:o * rows + first + count] = land[o]
        win[BELOW * rows + first:BELOW * rows + first + count] = sol[...]

    arrive(at_item[1])
    for i in range(half):
        serve(0, i)
    arrive(at_item[2])
    serve_rest(0)
    fill(land0, sol0, 0)

    for p in range(FIRST[1], LAST[1] + 1):
        if p == half:
            arrive(half)
        if p > 2:
            arrive(at_item[p])
        i = p - FIRST[1]
        sol1[i] = keep(p, 1, solve(p), sol0[p] if p <= LAST[0] else None)
        own_hops(1, i, start)
        serve(1, i)
    serve_rest(1)
    fill(land1, sol1, FIRST[1])

    for p in range(FIRST[2], LAST[2] + 1):
        if p == LAST[2]:
            arrive(at_item[p])
        i = p - FIRST[2]
        sol2[i] = keep(p, 2, solve(p), sol1[p - FIRST[1]] if p <= LAST[1] else None)
        own_hops(2, i, start)
        serve(2, i)
    arrive(at_item[rows - 1])
    serve_rest(2)
    fill(land2, sol2, FIRST[2])

    fin[0] = sol0[0]
    fin[1] = sol1[0]
    for p in range(FIRST[2], FIRST[3]):
        fin[p] = sol2[p - FIRST[2]]
    for p in range(FIRST[3], rows):
        fin[p] = keep(p, 3, solve(p), sol2[p - FIRST[2]] if p <= LAST[2] else None)
    for r in range(rows):
        out_ref[r] = fin[rank[BELOW * rows + r]]

    for i in range(len(items)):
        send_c(i).wait_send()
        send_f(i).wait_send()

    each_up(lambda d: send_lvl(d).wait_send())
    for v in range(BELOW):
        for i in range(sols[v].shape[0]):
            for hops in (own_hops, side_hops, up_hops):
                hops(v, i, lambda copy: copy.wait_send())


def per_device(n, right_side, off_blocks, diag_inverse, block_level, block_columns):
    rows, kk, part, bs = off_blocks.shape
    samples = right_side.shape[1]
    vmem = pl.BlockSpec(memory_space=pltpu.VMEM)
    smem = pl.BlockSpec(memory_space=pltpu.SMEM)
    tile = (samples, bs)
    counts = [b - a + 1 for a, b in zip(FIRST, LAST)]
    items = rows + 1
    dma = pltpu.SemaphoreType.DMA
    return pl.pallas_call(
        functools.partial(kernel, n),
        out_shape=jax.ShapeDtypeStruct(right_side.shape, jnp.bfloat16),
        in_specs=[smem, smem, vmem, vmem, vmem, vmem],
        out_specs=vmem,
        scratch_shapes=[
            pltpu.VMEM((rows - 1, 4 * part, kk * bs), jnp.bfloat16),
            pltpu.VMEM((rows, 4 * part, bs), jnp.bfloat16),
            pltpu.VMEM((REACH * rows,) + tile, jnp.bfloat16),
            pltpu.VMEM((BELOW, counts[0]) + tile, jnp.bfloat16),
            pltpu.VMEM((BELOW, counts[1]) + tile, jnp.bfloat16),
            pltpu.VMEM((BELOW, counts[2]) + tile, jnp.bfloat16),
            pltpu.VMEM((counts[0],) + tile, jnp.bfloat16),
            pltpu.VMEM((counts[1],) + tile, jnp.bfloat16),
            pltpu.VMEM((counts[2],) + tile, jnp.bfloat16),
            pltpu.VMEM((rows,) + tile, jnp.bfloat16),
            pltpu.VMEM((BELOW, rows, 128), jnp.int32),
            pltpu.SMEM((BELOW, rows, 128), jnp.int32),
            pltpu.SMEM((REACH * rows,), jnp.int32),
            pltpu.SMEM((rows,), jnp.int32),
            pltpu.SMEM((rows,), jnp.int32),
            dma((BELOW,)), dma((BELOW,)), dma,
            dma((items,)), dma((items,)), dma((items,)), dma((items,)), dma((items,)), dma((items,)),
            dma((counts[0], 4)), dma((counts[0], BELOW)),
            dma((counts[1], 4)), dma((counts[1], BELOW)),
            dma((counts[2], 4)), dma((counts[2], BELOW)),
        ],
        compiler_params=pltpu.CompilerParams(
            collective_id=0, has_side_effects=True, vmem_limit_bytes=48 * 2 ** 20),
    )(
        block_level, block_columns,
        jnp.broadcast_to(block_level[:, None], (rows, 128)),
        right_side, off_blocks, diag_inverse,
    )


def solution(mesh):
    return jax.shard_map(
        functools.partial(per_device, mesh.shape["rows"]),
        mesh=mesh,
        in_specs=(
            P("rows", "rhs", None),
            P("rows", None, "rhs", None),
            P("rows", "rhs", None),
            P("rows"),
            P("rows", None),
        ),
        out_specs=P("rows", "rhs", None),
        check_vma=False,
    )
```

```python
import functools

import jax
import jax.numpy as jnp
from jax import lax
from jax.experimental import pallas as pl
from jax.experimental.pallas import tpu as pltpu
from jax.sharding import PartitionSpec as P

REACH = 4
BELOW = REACH - 1
MESH = pl.DeviceIdType.MESH
FIRST = (0, 1, 2, 4)
LAST = (3, 5, 6, 7)
COUNTS = (4, 5, 4)
BASE = (0, 4, 9, 13)
HELD = 13
AHEAD = 3


def nt(a, b):
    return lax.dot_general(a, b, (((1,), (1,)), ((), ())), preferred_element_type=jnp.float32)


def kernel(
    n, level_ref, cols_ref, right_ref, off_ref, diag_ref, out_ref,
    fac, fac_last, inv, win, land0, land1, land2, sol0, sol1, sol2, lvl_ref, lvl_in, lvl_s, slot, perm,
    lvl_send, lvl_recv, lvl_sem, x_send, x_recv, c_send, c_recv, f_send, f_recv,
    w0_send, w0_recv, w1_send, w1_recv, w2_send, w2_recv,
):
    rows, kk, part, bs = off_ref.shape
    me, mine = lax.axis_index("rows"), lax.axis_index("rhs")
    core = mine + 1 - 2 * lax.rem(mine, 2)
    across = lax.rem(mine + 2, 4)

    lvl_in[...] = jnp.zeros_like(lvl_in)
    for r in range(rows):
        lvl_ref[r:r + 1, :] = jnp.full((1, lvl_ref.shape[1]), level_ref[r], jnp.int32)
    barrier = pltpu.get_barrier_semaphore()
    for other in (core, across):
        pl.semaphore_signal(barrier, inc=1, device_id=(me, other), device_id_type=MESH)
    for d in range(1, REACH):
        @pl.when(me + d < n)
        def _():
            pl.semaphore_signal(barrier, inc=1, device_id=(me + d, mine), device_id_type=MESH)

        @pl.when(me >= d)
        def _():
            pl.semaphore_signal(barrier, inc=1, device_id=(me - d, mine), device_id_type=MESH)

    own = [level_ref[r] for r in range(rows)]

    def ranked(levels, base):
        out = []
        lower = jnp.int32(0)
        for r in range(rows):
            lower += (levels[r] < 2).astype(jnp.int32)
        for r in range(rows):
            before = jnp.int32(0)
            for q in range(rows):
                if q < r:
                    before += (levels[q] <= levels[r]).astype(jnp.int32)
                elif q > r:
                    before += (levels[q] < levels[r]).astype(jnp.int32)
            at = jnp.where(levels[r] == 0, before, before - FIRST[1] + BASE[1])
            at = jnp.where(levels[r] == 2, before - lower + BASE[2], at)
            at = jnp.where(levels[r] == 3, before - FIRST[3] + BASE[3], at)
            slot[base * rows + r] = jnp.clip(at + base * HELD, 0, win.shape[0] - 1)
            out.append(before)
        return out, lower

    own_rank, lower2 = ranked(own, BELOW)
    where = []
    for p in range(rows):
        at = jnp.int32(0)
        for r in range(rows):
            at += jnp.where(own_rank[r] == p, r, 0)
        perm[p] = at
        where.append(at)

    def span(who):
        return pl.ds(pl.multiple_of(who * part, part), part)

    def stage_diag(p):
        inv[p, span(mine), :] = diag_ref[where[p]]

    def stage_off(p):
        for k in range(kk):
            if p == rows - 1:
                fac_last[span(mine), k * bs:(k + 1) * bs] = off_ref[where[p], k]
            else:
                fac[p - 1, span(mine), k * bs:(k + 1) * bs] = off_ref[where[p], k]

    half = rows // 2
    early = LAST[1] + 1
    items = [("d", (0, half))] + [("o", p) for p in range(1, half)] + [("d", (half, early))]
    items += [("o", p) for p in range(half, early)] + [("d", (early, rows))] + [("o", p) for p in range(early, rows)]

    def piece(item, who):
        kind, at = item
        if kind == "d":
            return inv.at[at[0]:at[1], span(who), :]
        if at == rows - 1:
            return fac_last.at[span(who), :]
        return fac.at[at - 1, span(who), :]

    def send_x(i):
        return pltpu.make_async_remote_copy(
            piece(items[i], mine), piece(items[i], mine), x_send.at[i], x_recv.at[i],
            device_id=(me, across), device_id_type=MESH)

    def send_c(i):
        return pltpu.make_async_remote_copy(
            piece(items[i], mine), piece(items[i], mine), c_send.at[i], c_recv.at[i],
            device_id=(me, core), device_id_type=MESH)

    def send_f(i):
        return pltpu.make_async_remote_copy(
            piece(items[i], across), piece(items[i], across), f_send.at[i], f_recv.at[i],
            device_id=(me, core), device_id_type=MESH)

    def issue(i):
        if i < len(items):
            send_x(i).start()
            send_c(i).start()

    def arrive(i):
        send_x(i).wait_recv()
        send_f(i).start()
        send_x(i).wait_send()
        issue(i + AHEAD)
        send_c(i).wait_recv()
        send_f(i).wait_recv()

    for p in range(rows):
        stage_diag(p)
        if p > 0:
            stage_off(p)

    greeted = jnp.int32(2)
    for d in range(1, REACH):
        greeted += (me + d < n).astype(jnp.int32) + (me >= d).astype(jnp.int32)
    pl.semaphore_wait(barrier, greeted)

    for i in range(AHEAD):
        issue(i)

    def send_lvl(d):
        return pltpu.make_async_remote_copy(
            lvl_ref, lvl_in.at[BELOW - d], lvl_send.at[d - 1], lvl_recv.at[d - 1],
            device_id=(me + d, mine), device_id_type=MESH)

    def each_up(what):
        for d in range(1, REACH):
            @pl.when(me + d < n)
            def _():
                what(d)

    def each_down(what):
        for d in range(1, REACH):
            @pl.when(me >= d)
            def _():
                what(d)

    even = lax.rem(me, 2) == 0
    odd = lax.rem(me, 2) == 1
    sols, lands = (sol0, sol1, sol2), (land0, land1, land2)
    hop_send, hop_recv = (w0_send, w1_send, w2_send), (w0_recv, w1_recv, w2_recv)
    OWN_UP, OWN_SIDE, PASS_SIDE, PASS_UP = range(4)

    def hop(v, i, way, to, d):
        src = sols[v].at[i]
        if way == PASS_SIDE:
            src = lands[v].at[BELOW - 2, i]
        if way == PASS_UP:
            src = lands[v].at[BELOW - 1, i]
        return pltpu.make_async_remote_copy(
            src, lands[v].at[BELOW - d, i], hop_send[v].at[i, way], hop_recv[v].at[i, d - 1],
            device_id=(to, mine), device_id_type=MESH)

    def landed(v, i, d):
        hop(v, i, OWN_UP, me, d).wait_recv()

    def own_hops(v, i, what):
        @pl.when(me + 2 < n)
        def _():
            what(hop(v, i, OWN_UP, me + 2, 2))

        @pl.when(even)
        def _():
            what(hop(v, i, OWN_SIDE, me + 1, 1))

    def side_hops(v, i, what):
        @pl.when(even & (me >= 2))
        def _():
            what(hop(v, i, PASS_SIDE, me + 1, 3))

        @pl.when(odd & (me >= 2))
        def _():
            what(hop(v, i, PASS_SIDE, me - 1, 1))

    def up_hops(v, i, what):
        @pl.when(even & (me >= 2) & (me + 2 < n))
        def _():
            what(hop(v, i, PASS_UP, me + 2, 3))

    def start(copy):
        copy.start()

    def first_leg(v, i):
        @pl.when(me >= 2)
        def _():
            landed(v, i, 2)
        side_hops(v, i, start)

    def second_leg(v, i):
        @pl.when(me >= 1)
        def _():
            landed(v, i, 1)
        up_hops(v, i, start)

    def third_leg(v, i):
        @pl.when(me >= 3)
        def _():
            landed(v, i, 3)

    def serve(v, i):
        count = sols[v].shape[0]
        for leg, late in ((first_leg, 1), (second_leg, 2), (third_leg, 3)):
            if 0 <= i - late < count:
                leg(v, i - late)

    def serve_rest(v):
        count = sols[v].shape[0]
        for i in range(count, count + 3):
            serve(v, i)

    each_up(lambda d: send_lvl(d).start())

    at_item = {p: items.index(("o", p)) for p in range(1, rows)}
    arrive(0)
    for p in range(half):
        sol0[p] = nt(right_ref[where[p]], inv[p]).astype(jnp.bfloat16)
        own_hops(0, p, start)

    each_down(lambda d: send_lvl(d).wait_recv())
    fetch = pltpu.make_async_copy(lvl_in, lvl_s, lvl_sem)
    fetch.start()
    fetch.wait()
    for o in range(BELOW):
        ranked([lvl_s[o, r, 0] for r in range(rows)], o)

    def solve(p, factor, inverse):
        row = perm[p]
        taken = []
        for k in range(kk):
            at = cols_ref[row, k] - (me - BELOW) * rows
            taken.append(win[slot[jnp.clip(at, 0, REACH * rows - 1)]])
        contribution = nt(jnp.concatenate(taken, axis=1), factor)
        residue = (right_ref[row].astype(jnp.float32) - contribution).astype(jnp.bfloat16)
        return nt(residue, inverse).astype(jnp.bfloat16)

    def fill(v):
        for d in range(1, REACH):
            o = (BELOW - d) * HELD + BASE[v]
            win[o:o + COUNTS[v]] = lands[v][BELOW - d]
        o = BELOW * HELD + BASE[v]
        win[o:o + COUNTS[v]] = sols[v][...]

    arrive(at_item[1])
    for i in range(half):
        serve(0, i)
    arrive(at_item[2])
    serve_rest(0)
    fill(0)

    for p in range(FIRST[1], LAST[1] + 1):
        if p == half:
            arrive(items.index(("d", (half, early))))
        if p > 2:
            arrive(at_item[p])
        i = p - FIRST[1]
        sol1[i] = solve(p, fac[p - 1], inv[p])
        own_hops(1, i, start)
        serve(1, i)
    serve_rest(1)
    fill(1)

    arrive(items.index(("d", (early, rows))))
    for p in range(early, rows - 1):
        arrive(at_item[p])
    for i in range(COUNTS[2]):
        p = jnp.clip(lower2 + i, FIRST[2], LAST[2])
        sol2[i] = solve(p, fac[p - 1], inv[p])
        own_hops(2, i, start)
        serve(2, i)
    arrive(at_item[rows - 1])
    serve_rest(2)
    fill(2)

    o = BELOW * HELD + BASE[3] - FIRST[3]
    for p in range(FIRST[3], rows):
        win[o + p] = solve(p, fac_last[...] if p == rows - 1 else fac[p - 1], inv[p])
    for r in range(rows):
        out_ref[r] = win[slot[BELOW * rows + r]]

    for i in range(len(items)):
        send_c(i).wait_send()
        send_f(i).wait_send()

    each_up(lambda d: send_lvl(d).wait_send())
    for v in range(BELOW):
        for i in range(sols[v].shape[0]):
            for hops in (own_hops, side_hops, up_hops):
                hops(v, i, lambda copy: copy.wait_send())


def per_device(n, right_side, off_blocks, diag_inverse, block_level, block_columns):
    rows, kk, part, bs = off_blocks.shape
    samples = right_side.shape[1]
    vmem = pl.BlockSpec(memory_space=pltpu.VMEM)
    smem = pl.BlockSpec(memory_space=pltpu.SMEM)
    tile = (samples, bs)
    counts = COUNTS
    items = rows + 2
    dma = pltpu.SemaphoreType.DMA
    return pl.pallas_call(
        functools.partial(kernel, n),
        out_shape=jax.ShapeDtypeStruct(right_side.shape, jnp.bfloat16),
        in_specs=[smem, smem, vmem, vmem, vmem],
        out_specs=vmem,
        scratch_shapes=[
            pltpu.VMEM((rows - 2, 4 * part, kk * bs), jnp.bfloat16),
            pltpu.VMEM((4 * part, kk * bs), jnp.bfloat16),
            pltpu.VMEM((rows, 4 * part, bs), jnp.bfloat16),
            pltpu.VMEM((REACH * HELD + rows - FIRST[3],) + tile, jnp.bfloat16),
            pltpu.VMEM((BELOW, counts[0]) + tile, jnp.bfloat16),
            pltpu.VMEM((BELOW, counts[1]) + tile, jnp.bfloat16),
            pltpu.VMEM((BELOW, counts[2]) + tile, jnp.bfloat16),
            pltpu.VMEM((counts[0],) + tile, jnp.bfloat16),
            pltpu.VMEM((counts[1],) + tile, jnp.bfloat16),
            pltpu.VMEM((counts[2],) + tile, jnp.bfloat16),
            pltpu.VMEM((rows, 128), jnp.int32),
            pltpu.VMEM((BELOW, rows, 128), jnp.int32),
            pltpu.SMEM((BELOW, rows, 128), jnp.int32),
            pltpu.SMEM((REACH * rows,), jnp.int32),
            pltpu.SMEM((rows,), jnp.int32),
            dma((BELOW,)), dma((BELOW,)), dma,
            dma((items,)), dma((items,)), dma((items,)), dma((items,)), dma((items,)), dma((items,)),
            dma((counts[0], 4)), dma((counts[0], BELOW)),
            dma((counts[1], 4)), dma((counts[1], BELOW)),
            dma((counts[2], 4)), dma((counts[2], BELOW)),
        ],
        compiler_params=pltpu.CompilerParams(
            collective_id=0, has_side_effects=True, vmem_limit_bytes=48 * 2 ** 20),
    )(
        block_level, block_columns, right_side, off_blocks, diag_inverse,
    )


def solution(mesh):
    return jax.shard_map(
        functools.partial(per_device, mesh.shape["rows"]),
        mesh=mesh,
        in_specs=(
            P("rows", "rhs", None),
            P("rows", None, "rhs", None),
            P("rows", "rhs", None),
            P("rows"),
            P("rows", None),
        ),
        out_specs=P("rows", "rhs", None),
        check_vma=False,
    )
```

```python
import functools

import jax
import jax.numpy as jnp
from jax import lax
from jax.experimental import pallas as pl
from jax.experimental.pallas import tpu as pltpu
from jax.sharding import PartitionSpec as P

REACH = 4
BELOW = REACH - 1
MESH = pl.DeviceIdType.MESH
FIRST = (0, 1, 2, 4)
LAST = (3, 5, 6, 7)
COUNTS = (4, 5, 4)
BASE = (0, 4, 9, 13)
HELD = 13
AHEAD = 3


def nt(a, b):
    return lax.dot_general(a, b, (((1,), (1,)), ((), ())), preferred_element_type=jnp.float32)


def kernel(
    n, level_ref, cols_ref, right_in, off_in, diag_in, out_ref,
    right_ref, off_ref, diag_ref, in_sem, fac, fac_last, inv, win, land0, land1, land2, sol0, sol1, sol2, sol3, lvl_ref, lvl_in, lvl_s, slot, perm,
    lvl_send, lvl_recv, lvl_sem, x_send, x_recv, c_send, c_recv, f_send, f_recv,
    w0_send, w0_recv, w1_send, w1_recv, w2_send, w2_recv,
):
    rows, kk, part, bs = off_ref.shape
    me, mine = lax.axis_index("rows"), lax.axis_index("rhs")
    core = mine + 1 - 2 * lax.rem(mine, 2)
    across = lax.rem(mine + 2, 4)

    fetches = [
        pltpu.make_async_copy(src, dst, in_sem.at[i])
        for i, (src, dst) in enumerate([(diag_in, diag_ref), (off_in, off_ref), (right_in, right_ref)])
    ]
    for copy in fetches:
        copy.start()
    lvl_in[...] = jnp.zeros_like(lvl_in)
    for r in range(rows):
        lvl_ref[r:r + 1, :] = jnp.full((1, lvl_ref.shape[1]), level_ref[r], jnp.int32)
    barrier = pltpu.get_barrier_semaphore()
    for other in (core, across):
        pl.semaphore_signal(barrier, inc=1, device_id=(me, other), device_id_type=MESH)
    for d in range(1, REACH):
        @pl.when(me + d < n)
        def _():
            pl.semaphore_signal(barrier, inc=1, device_id=(me + d, mine), device_id_type=MESH)

        @pl.when(me >= d)
        def _():
            pl.semaphore_signal(barrier, inc=1, device_id=(me - d, mine), device_id_type=MESH)

    own = [level_ref[r] for r in range(rows)]

    def ranked(levels, base):
        out = []
        lower = jnp.int32(0)
        for r in range(rows):
            lower += (levels[r] < 2).astype(jnp.int32)
        for r in range(rows):
            before = jnp.int32(0)
            for q in range(rows):
                if q < r:
                    before += (levels[q] <= levels[r]).astype(jnp.int32)
                elif q > r:
                    before += (levels[q] < levels[r]).astype(jnp.int32)
            at = jnp.where(levels[r] == 0, before, before - FIRST[1] + BASE[1])
            at = jnp.where(levels[r] == 2, before - lower + BASE[2], at)
            at = jnp.where(levels[r] == 3, before - FIRST[3] + BASE[3], at)
            slot[base * rows + r] = jnp.clip(at + base * HELD, 0, win.shape[0] - 1)
            out.append(before)
        return out, lower

    own_rank, lower2 = ranked(own, BELOW)
    where = []
    for p in range(rows):
        at = jnp.int32(0)
        for r in range(rows):
            at += jnp.where(own_rank[r] == p, r, 0)
        perm[p] = at
        where.append(at)

    def span(who):
        return pl.ds(pl.multiple_of(who * part, part), part)

    def stage_diag(p):
        inv[p, span(mine), :] = diag_ref[where[p]]

    def stage_off(p):
        for k in range(kk):
            if p == rows - 1:
                fac_last[span(mine), k * bs:(k + 1) * bs] = off_ref[where[p], k]
            else:
                fac[p - 1, span(mine), k * bs:(k + 1) * bs] = off_ref[where[p], k]

    half = rows // 2
    early = LAST[1] + 1
    items = [("d", (0, half))] + [("o", p) for p in range(1, half)] + [("d", (half, early))]
    items += [("o", p) for p in range(half, early)] + [("d", (early, rows))] + [("o", p) for p in range(early, rows)]

    def piece(item, who):
        kind, at = item
        if kind == "d":
            return inv.at[at[0]:at[1], span(who), :]
        if at == rows - 1:
            return fac_last.at[span(who), :]
        return fac.at[at - 1, span(who), :]

    def send_x(i):
        return pltpu.make_async_remote_copy(
            piece(items[i], mine), piece(items[i], mine), x_send.at[i], x_recv.at[i],
            device_id=(me, across), device_id_type=MESH)

    def send_c(i):
        return pltpu.make_async_remote_copy(
            piece(items[i], mine), piece(items[i], mine), c_send.at[i], c_recv.at[i],
            device_id=(me, core), device_id_type=MESH)

    def send_f(i):
        return pltpu.make_async_remote_copy(
            piece(items[i], across), piece(items[i], across), f_send.at[i], f_recv.at[i],
            device_id=(me, core), device_id_type=MESH)

    def issue(i):
        if i < len(items):
            send_x(i).start()
            send_c(i).start()

    def arrive(i):
        send_x(i).wait_recv()
        send_f(i).start()
        send_x(i).wait_send()
        issue(i + AHEAD)
        send_c(i).wait_recv()
        send_f(i).wait_recv()

    fetches[0].wait()
    for p in range(rows):
        stage_diag(p)

    greeted = jnp.int32(2)
    for d in range(1, REACH):
        greeted += (me + d < n).astype(jnp.int32) + (me >= d).astype(jnp.int32)
    pl.semaphore_wait(barrier, greeted)

    issue(0)
    fetches[1].wait()
    for p in range(1, rows):
        stage_off(p)
        if p < AHEAD:
            issue(p)
    fetches[2].wait()

    def send_lvl(d):
        return pltpu.make_async_remote_copy(
            lvl_ref, lvl_in.at[BELOW - d], lvl_send.at[d - 1], lvl_recv.at[d - 1],
            device_id=(me + d, mine), device_id_type=MESH)

    def each_up(what):
        for d in range(1, REACH):
            @pl.when(me + d < n)
            def _():
                what(d)

    def each_down(what):
        for d in range(1, REACH):
            @pl.when(me >= d)
            def _():
                what(d)

    even = lax.rem(me, 2) == 0
    odd = lax.rem(me, 2) == 1
    sols, lands = (sol0, sol1, sol2), (land0, land1, land2)
    hop_send, hop_recv = (w0_send, w1_send, w2_send), (w0_recv, w1_recv, w2_recv)
    OWN_UP, OWN_SIDE, PASS_SIDE, PASS_UP = range(4)

    def hop(v, i, way, to, d):
        src = sols[v].at[i]
        if way == PASS_SIDE:
            src = lands[v].at[BELOW - 2, i]
        if way == PASS_UP:
            src = lands[v].at[BELOW - 1, i]
        return pltpu.make_async_remote_copy(
            src, lands[v].at[BELOW - d, i], hop_send[v].at[i, way], hop_recv[v].at[i, d - 1],
            device_id=(to, mine), device_id_type=MESH)

    def landed(v, i, d):
        hop(v, i, OWN_UP, me, d).wait_recv()

    def own_hops(v, i, what):
        @pl.when(me + 2 < n)
        def _():
            what(hop(v, i, OWN_UP, me + 2, 2))

        @pl.when(even)
        def _():
            what(hop(v, i, OWN_SIDE, me + 1, 1))

    def side_hops(v, i, what):
        @pl.when(even & (me >= 2))
        def _():
            what(hop(v, i, PASS_SIDE, me + 1, 3))

        @pl.when(odd & (me >= 2))
        def _():
            what(hop(v, i, PASS_SIDE, me - 1, 1))

    def up_hops(v, i, what):
        @pl.when(even & (me >= 2) & (me + 2 < n))
        def _():
            what(hop(v, i, PASS_UP, me + 2, 3))

    def start(copy):
        copy.start()

    def first_leg(v, i):
        @pl.when(me >= 2)
        def _():
            landed(v, i, 2)
        side_hops(v, i, start)

    def second_leg(v, i):
        @pl.when(me >= 1)
        def _():
            landed(v, i, 1)
        up_hops(v, i, start)

    def third_leg(v, i):
        @pl.when(me >= 3)
        def _():
            landed(v, i, 3)

    def serve(v, i):
        count = sols[v].shape[0]
        for leg, late in ((first_leg, 1), (second_leg, 2), (third_leg, 3)):
            if 0 <= i - late < count:
                leg(v, i - late)

    def serve_rest(v):
        count = sols[v].shape[0]
        for i in range(count, count + 3):
            serve(v, i)

    each_up(lambda d: send_lvl(d).start())

    at_item = {p: items.index(("o", p)) for p in range(1, rows)}
    arrive(0)
    for p in range(half):
        sol0[p] = nt(right_ref[where[p]], inv[p]).astype(jnp.bfloat16)
        own_hops(0, p, start)

    each_down(lambda d: send_lvl(d).wait_recv())
    fetch = pltpu.make_async_copy(lvl_in, lvl_s, lvl_sem)
    fetch.start()
    fetch.wait()
    for o in range(BELOW):
        ranked([lvl_s[o, r, 0] for r in range(rows)], o)

    def solve(p, factor, inverse):
        row = perm[p]
        taken = []
        for k in range(kk):
            at = cols_ref[row, k] - (me - BELOW) * rows
            taken.append(win[slot[jnp.clip(at, 0, REACH * rows - 1)]])
        contribution = nt(jnp.concatenate(taken, axis=1), factor)
        residue = (right_ref[row].astype(jnp.float32) - contribution).astype(jnp.bfloat16)
        return nt(residue, inverse).astype(jnp.bfloat16)

    def fill(v):
        for d in range(1, REACH):
            o = (BELOW - d) * HELD + BASE[v]
            win[o:o + COUNTS[v]] = lands[v][BELOW - d]
        o = BELOW * HELD + BASE[v]
        win[o:o + COUNTS[v]] = sols[v][...]

    arrive(at_item[1])
    for i in range(half):
        serve(0, i)
    arrive(at_item[2])
    serve_rest(0)
    fill(0)

    for p in range(FIRST[1], LAST[1] + 1):
        if p == half:
            arrive(items.index(("d", (half, early))))
        if p > 2:
            arrive(at_item[p])
        i = p - FIRST[1]
        sol1[i] = solve(p, fac[p - 1], inv[p])
        own_hops(1, i, start)
        serve(1, i)
    serve_rest(1)
    fill(1)

    arrive(items.index(("d", (early, rows))))
    for p in range(early, rows - 1):
        arrive(at_item[p])
    for i in range(COUNTS[2]):
        p = jnp.clip(lower2 + i, FIRST[2], LAST[2])
        sol2[i] = solve(p, fac[p - 1], inv[p])
        own_hops(2, i, start)
        serve(2, i)
    arrive(at_item[rows - 1])
    serve_rest(2)
    fill(2)

    for p in range(FIRST[3], rows):
        sol3[p - FIRST[3]] = solve(p, fac_last[...] if p == rows - 1 else fac[p - 1], inv[p])
    win[BELOW * HELD + BASE[3]:] = sol3[...]
    for r in range(rows):
        out_ref[r] = win[slot[BELOW * rows + r]]

    for i in range(len(items)):
        send_c(i).wait_send()
        send_f(i).wait_send()

    each_up(lambda d: send_lvl(d).wait_send())
    for v in range(BELOW):
        for i in range(sols[v].shape[0]):
            for hops in (own_hops, side_hops, up_hops):
                hops(v, i, lambda copy: copy.wait_send())


def per_device(n, right_side, off_blocks, diag_inverse, block_level, block_columns):
    rows, kk, part, bs = off_blocks.shape
    samples = right_side.shape[1]
    vmem = pl.BlockSpec(memory_space=pltpu.VMEM)
    smem = pl.BlockSpec(memory_space=pltpu.SMEM)
    anywhere = pl.BlockSpec(memory_space=pl.ANY)
    tile = (samples, bs)
    counts = COUNTS
    items = rows + 2
    dma = pltpu.SemaphoreType.DMA
    return pl.pallas_call(
        functools.partial(kernel, n),
        out_shape=jax.ShapeDtypeStruct(right_side.shape, jnp.bfloat16),
        in_specs=[smem, smem, anywhere, anywhere, anywhere],
        out_specs=vmem,
        scratch_shapes=[
            pltpu.VMEM(right_side.shape, jnp.bfloat16),
            pltpu.VMEM(off_blocks.shape, jnp.bfloat16),
            pltpu.VMEM(diag_inverse.shape, jnp.bfloat16),
            dma((3,)),
            pltpu.VMEM((rows - 2, 4 * part, kk * bs), jnp.bfloat16),
            pltpu.VMEM((4 * part, kk * bs), jnp.bfloat16),
            pltpu.VMEM((rows, 4 * part, bs), jnp.bfloat16),
            pltpu.VMEM((REACH * HELD + rows - FIRST[3],) + tile, jnp.bfloat16),
            pltpu.VMEM((BELOW, counts[0]) + tile, jnp.bfloat16),
            pltpu.VMEM((BELOW, counts[1]) + tile, jnp.bfloat16),
            pltpu.VMEM((BELOW, counts[2]) + tile, jnp.bfloat16),
            pltpu.VMEM((counts[0],) + tile, jnp.bfloat16),
            pltpu.VMEM((counts[1],) + tile, jnp.bfloat16),
            pltpu.VMEM((counts[2],) + tile, jnp.bfloat16),
            pltpu.VMEM((rows - FIRST[3],) + tile, jnp.bfloat16),
            pltpu.VMEM((rows, 128), jnp.int32),
            pltpu.VMEM((BELOW, rows, 128), jnp.int32),
            pltpu.SMEM((BELOW, rows, 128), jnp.int32),
            pltpu.SMEM((REACH * rows,), jnp.int32),
            pltpu.SMEM((rows,), jnp.int32),
            dma((BELOW,)), dma((BELOW,)), dma,
            dma((items,)), dma((items,)), dma((items,)), dma((items,)), dma((items,)), dma((items,)),
            dma((counts[0], 4)), dma((counts[0], BELOW)),
            dma((counts[1], 4)), dma((counts[1], BELOW)),
            dma((counts[2], 4)), dma((counts[2], BELOW)),
        ],
        compiler_params=pltpu.CompilerParams(
            collective_id=0, has_side_effects=True, vmem_limit_bytes=48 * 2 ** 20),
    )(
        block_level, block_columns, right_side, off_blocks, diag_inverse,
    )


def solution(mesh):
    return jax.shard_map(
        functools.partial(per_device, mesh.shape["rows"]),
        mesh=mesh,
        in_specs=(
            P("rows", "rhs", None),
            P("rows", None, "rhs", None),
            P("rows", "rhs", None),
            P("rows"),
            P("rows", None),
        ),
        out_specs=P("rows", "rhs", None),
        check_vma=False,
    )
```

```python
import functools

import jax
import jax.numpy as jnp
from jax import lax
from jax.experimental import pallas as pl
from jax.experimental.pallas import tpu as pltpu
from jax.sharding import PartitionSpec as P

REACH = 4
BELOW = REACH - 1
MESH = pl.DeviceIdType.MESH
FIRST = (0, 1, 2, 4)
LAST = (3, 5, 6, 7)
COUNTS = (4, 5, 4)
BASE = (0, 4, 9, 13)
HELD = 13
AHEAD = 5


def nt(a, b):
    return lax.dot_general(a, b, (((1,), (1,)), ((), ())), preferred_element_type=jnp.float32)


def kernel(
    n, level_ref, cols_ref, right_in, off_in, diag_in, out_ref,
    right_ref, off_ref, diag_ref, in_sem, fac, fac_last, inv, win, land0, land1, land2, sol0, sol1, sol2, sol3, lvl_ref, lvl_in, lvl_s, slot, perm,
    lvl_send, lvl_recv, lvl_sem, x_send, x_recv, c_send, c_recv, f_send, f_recv,
    w0_send, w0_recv, w1_send, w1_recv, w2_send, w2_recv,
):
    rows, kk, part, bs = off_ref.shape
    me, mine = lax.axis_index("rows"), lax.axis_index("rhs")
    core = mine + 1 - 2 * lax.rem(mine, 2)
    across = lax.rem(mine + 2, 4)

    fetches = [
        pltpu.make_async_copy(src, dst, in_sem.at[i])
        for i, (src, dst) in enumerate([(diag_in, diag_ref), (off_in, off_ref), (right_in, right_ref)])
    ]
    for copy in fetches:
        copy.start()
    lvl_in[...] = jnp.zeros_like(lvl_in)
    for r in range(rows):
        lvl_ref[r:r + 1, :] = jnp.full((1, lvl_ref.shape[1]), level_ref[r], jnp.int32)
    barrier = pltpu.get_barrier_semaphore()
    for other in (core, across):
        pl.semaphore_signal(barrier, inc=1, device_id=(me, other), device_id_type=MESH)
    for d in range(1, REACH):
        @pl.when(me + d < n)
        def _():
            pl.semaphore_signal(barrier, inc=1, device_id=(me + d, mine), device_id_type=MESH)

        @pl.when(me >= d)
        def _():
            pl.semaphore_signal(barrier, inc=1, device_id=(me - d, mine), device_id_type=MESH)

    own = [level_ref[r] for r in range(rows)]

    def ranked(levels, base):
        out = []
        lower = jnp.int32(0)
        for r in range(rows):
            lower += (levels[r] < 2).astype(jnp.int32)
        for r in range(rows):
            before = jnp.int32(0)
            for q in range(rows):
                if q < r:
                    before += (levels[q] <= levels[r]).astype(jnp.int32)
                elif q > r:
                    before += (levels[q] < levels[r]).astype(jnp.int32)
            at = jnp.where(levels[r] == 0, before, before - FIRST[1] + BASE[1])
            at = jnp.where(levels[r] == 2, before - lower + BASE[2], at)
            at = jnp.where(levels[r] == 3, before - FIRST[3] + BASE[3], at)
            slot[base * rows + r] = jnp.clip(at + base * HELD, 0, win.shape[0] - 1)
            out.append(before)
        return out, lower

    own_rank, lower2 = ranked(own, BELOW)
    where = []
    for p in range(rows):
        at = jnp.int32(0)
        for r in range(rows):
            at += jnp.where(own_rank[r] == p, r, 0)
        perm[p] = at
        where.append(at)

    def span(who):
        return pl.ds(pl.multiple_of(who * part, part), part)

    def stage_diag(p):
        inv[p, span(mine), :] = diag_ref[where[p]]

    def stage_off(p):
        for k in range(kk):
            if p == rows - 1:
                fac_last[span(mine), k * bs:(k + 1) * bs] = off_ref[where[p], k]
            else:
                fac[p - 1, span(mine), k * bs:(k + 1) * bs] = off_ref[where[p], k]

    half = rows // 2
    early = LAST[1] + 1
    items = [("d", (0, half))] + [("o", p) for p in range(1, half)] + [("d", (half, early))]
    items += [("o", p) for p in range(half, early)] + [("d", (early, rows))] + [("o", p) for p in range(early, rows)]

    def piece(item, who):
        kind, at = item
        if kind == "d":
            return inv.at[at[0]:at[1], span(who), :]
        if at == rows - 1:
            return fac_last.at[span(who), :]
        return fac.at[at - 1, span(who), :]

    def send_x(i):
        return pltpu.make_async_remote_copy(
            piece(items[i], mine), piece(items[i], mine), x_send.at[i], x_recv.at[i],
            device_id=(me, across), device_id_type=MESH)

    def send_c(i):
        return pltpu.make_async_remote_copy(
            piece(items[i], mine), piece(items[i], mine), c_send.at[i], c_recv.at[i],
            device_id=(me, core), device_id_type=MESH)

    def send_f(i):
        return pltpu.make_async_remote_copy(
            piece(items[i], across), piece(items[i], across), f_send.at[i], f_recv.at[i],
            device_id=(me, core), device_id_type=MESH)

    def issue(i):
        if i < len(items):
            send_x(i).start()
            send_c(i).start()

    def arrive(i):
        send_x(i).wait_recv()
        send_f(i).start()
        send_x(i).wait_send()
        issue(i + AHEAD)
        send_c(i).wait_recv()
        send_f(i).wait_recv()

    fetches[0].wait()
    for p in range(rows):
        stage_diag(p)

    greeted = jnp.int32(2)
    for d in range(1, REACH):
        greeted += (me + d < n).astype(jnp.int32) + (me >= d).astype(jnp.int32)
    pl.semaphore_wait(barrier, greeted)

    issue(0)
    fetches[1].wait()
    staged = 0
    for i in range(1, AHEAD):
        kind, at = items[i]
        if kind == "o":
            stage_off(at)
            staged = at
        issue(i)
    for p in range(staged + 1, rows):
        stage_off(p)
    fetches[2].wait()

    def send_lvl(d):
        return pltpu.make_async_remote_copy(
            lvl_ref, lvl_in.at[BELOW - d], lvl_send.at[d - 1], lvl_recv.at[d - 1],
            device_id=(me + d, mine), device_id_type=MESH)

    def each_up(what):
        for d in range(1, REACH):
            @pl.when(me + d < n)
            def _():
                what(d)

    def each_down(what):
        for d in range(1, REACH):
            @pl.when(me >= d)
            def _():
                what(d)

    even = lax.rem(me, 2) == 0
    odd = lax.rem(me, 2) == 1
    sols, lands = (sol0, sol1, sol2), (land0, land1, land2)
    hop_send, hop_recv = (w0_send, w1_send, w2_send), (w0_recv, w1_recv, w2_recv)
    OWN_UP, OWN_SIDE, PASS_SIDE, PASS_UP = range(4)

    def hop(v, i, way, to, d):
        src = sols[v].at[i]
        if way == PASS_SIDE:
            src = lands[v].at[BELOW - 2, i]
        if way == PASS_UP:
            src = lands[v].at[BELOW - 1, i]
        return pltpu.make_async_remote_copy(
            src, lands[v].at[BELOW - d, i], hop_send[v].at[i, way], hop_recv[v].at[i, d - 1],
            device_id=(to, mine), device_id_type=MESH)

    def landed(v, i, d):
        hop(v, i, OWN_UP, me, d).wait_recv()

    def own_hops(v, i, what):
        @pl.when(me + 2 < n)
        def _():
            what(hop(v, i, OWN_UP, me + 2, 2))

        @pl.when(even)
        def _():
            what(hop(v, i, OWN_SIDE, me + 1, 1))

    def side_hops(v, i, what):
        @pl.when(even & (me >= 2))
        def _():
            what(hop(v, i, PASS_SIDE, me + 1, 3))

        @pl.when(odd & (me >= 2))
        def _():
            what(hop(v, i, PASS_SIDE, me - 1, 1))

    def up_hops(v, i, what):
        @pl.when(even & (me >= 2) & (me + 2 < n))
        def _():
            what(hop(v, i, PASS_UP, me + 2, 3))

    def start(copy):
        copy.start()

    def first_leg(v, i):
        @pl.when(me >= 2)
        def _():
            landed(v, i, 2)
        side_hops(v, i, start)

    def second_leg(v, i):
        @pl.when(me >= 1)
        def _():
            landed(v, i, 1)
        up_hops(v, i, start)

    def third_leg(v, i):
        @pl.when(me >= 3)
        def _():
            landed(v, i, 3)

    def serve(v, i):
        count = sols[v].shape[0]
        for leg, late in ((first_leg, 1), (second_leg, 2), (third_leg, 3)):
            if 0 <= i - late < count:
                leg(v, i - late)

    def serve_rest(v):
        count = sols[v].shape[0]
        for i in range(count, count + 3):
            serve(v, i)

    each_up(lambda d: send_lvl(d).start())

    at_item = {p: items.index(("o", p)) for p in range(1, rows)}
    arrive(0)
    for p in range(half):
        sol0[p] = nt(right_ref[where[p]], inv[p]).astype(jnp.bfloat16)
        own_hops(0, p, start)

    each_down(lambda d: send_lvl(d).wait_recv())
    fetch = pltpu.make_async_copy(lvl_in, lvl_s, lvl_sem)
    fetch.start()
    fetch.wait()
    for o in range(BELOW):
        ranked([lvl_s[o, r, 0] for r in range(rows)], o)

    def solve(p, factor, inverse):
        row = perm[p]
        taken = []
        for k in range(kk):
            at = cols_ref[row, k] - (me - BELOW) * rows
            taken.append(win[slot[jnp.clip(at, 0, REACH * rows - 1)]])
        contribution = nt(jnp.concatenate(taken, axis=1), factor)
        residue = (right_ref[row].astype(jnp.float32) - contribution).astype(jnp.bfloat16)
        return nt(residue, inverse).astype(jnp.bfloat16)

    def fill(v):
        for d in range(1, REACH):
            o = (BELOW - d) * HELD + BASE[v]
            win[o:o + COUNTS[v]] = lands[v][BELOW - d]
        o = BELOW * HELD + BASE[v]
        win[o:o + COUNTS[v]] = sols[v][...]

    arrive(at_item[1])
    for i in range(half):
        serve(0, i)
    arrive(at_item[2])
    serve_rest(0)
    fill(0)

    for p in range(FIRST[1], LAST[1] + 1):
        if p == half:
            arrive(items.index(("d", (half, early))))
        if p > 2:
            arrive(at_item[p])
        i = p - FIRST[1]
        sol1[i] = solve(p, fac[p - 1], inv[p])
        own_hops(1, i, start)
        serve(1, i)
    serve_rest(1)
    fill(1)

    arrive(items.index(("d", (early, rows))))
    for p in range(early, rows - 1):
        arrive(at_item[p])
    for i in range(COUNTS[2]):
        p = jnp.clip(lower2 + i, FIRST[2], LAST[2])
        sol2[i] = solve(p, fac[p - 1], inv[p])
        own_hops(2, i, start)
        serve(2, i)
    arrive(at_item[rows - 1])
    serve_rest(2)
    fill(2)

    for p in range(FIRST[3], rows):
        sol3[p - FIRST[3]] = solve(p, fac_last[...] if p == rows - 1 else fac[p - 1], inv[p])
    win[BELOW * HELD + BASE[3]:] = sol3[...]
    for r in range(rows):
        out_ref[r] = win[slot[BELOW * rows + r]]

    for i in range(len(items)):
        send_c(i).wait_send()
        send_f(i).wait_send()

    each_up(lambda d: send_lvl(d).wait_send())
    for v in range(BELOW):
        for i in range(sols[v].shape[0]):
            for hops in (own_hops, side_hops, up_hops):
                hops(v, i, lambda copy: copy.wait_send())


def per_device(n, right_side, off_blocks, diag_inverse, block_level, block_columns):
    rows, kk, part, bs = off_blocks.shape
    samples = right_side.shape[1]
    vmem = pl.BlockSpec(memory_space=pltpu.VMEM)
    smem = pl.BlockSpec(memory_space=pltpu.SMEM)
    anywhere = pl.BlockSpec(memory_space=pltpu.HBM)
    tile = (samples, bs)
    counts = COUNTS
    items = rows + 2
    dma = pltpu.SemaphoreType.DMA
    return pl.pallas_call(
        functools.partial(kernel, n),
        out_shape=jax.ShapeDtypeStruct(right_side.shape, jnp.bfloat16),
        in_specs=[smem, smem, anywhere, anywhere, anywhere],
        out_specs=vmem,
        scratch_shapes=[
            pltpu.VMEM(right_side.shape, jnp.bfloat16),
            pltpu.VMEM(off_blocks.shape, jnp.bfloat16),
            pltpu.VMEM(diag_inverse.shape, jnp.bfloat16),
            dma((3,)),
            pltpu.VMEM((rows - 2, 4 * part, kk * bs), jnp.bfloat16),
            pltpu.VMEM((4 * part, kk * bs), jnp.bfloat16),
            pltpu.VMEM((rows, 4 * part, bs), jnp.bfloat16),
            pltpu.VMEM((REACH * HELD + rows - FIRST[3],) + tile, jnp.bfloat16),
            pltpu.VMEM((BELOW, counts[0]) + tile, jnp.bfloat16),
            pltpu.VMEM((BELOW, counts[1]) + tile, jnp.bfloat16),
            pltpu.VMEM((BELOW, counts[2]) + tile, jnp.bfloat16),
            pltpu.VMEM((counts[0],) + tile, jnp.bfloat16),
            pltpu.VMEM((counts[1],) + tile, jnp.bfloat16),
            pltpu.VMEM((counts[2],) + tile, jnp.bfloat16),
            pltpu.VMEM((rows - FIRST[3],) + tile, jnp.bfloat16),
            pltpu.VMEM((rows, 128), jnp.int32),
            pltpu.VMEM((BELOW, rows, 128), jnp.int32),
            pltpu.SMEM((BELOW, rows, 128), jnp.int32),
            pltpu.SMEM((REACH * rows,), jnp.int32),
            pltpu.SMEM((rows,), jnp.int32),
            dma((BELOW,)), dma((BELOW,)), dma,
            dma((items,)), dma((items,)), dma((items,)), dma((items,)), dma((items,)), dma((items,)),
            dma((counts[0], 4)), dma((counts[0], BELOW)),
            dma((counts[1], 4)), dma((counts[1], BELOW)),
            dma((counts[2], 4)), dma((counts[2], BELOW)),
        ],
        compiler_params=pltpu.CompilerParams(
            collective_id=0, has_side_effects=True, vmem_limit_bytes=62 * 2 ** 20),
    )(
        block_level, block_columns, right_side, off_blocks, diag_inverse,
    )


def solution(mesh):
    return jax.shard_map(
        functools.partial(per_device, mesh.shape["rows"]),
        mesh=mesh,
        in_specs=(
            P("rows", "rhs", None),
            P("rows", None, "rhs", None),
            P("rows", "rhs", None),
            P("rows"),
            P("rows", None),
        ),
        out_specs=P("rows", "rhs", None),
        check_vma=False,
    )
```

```python
import functools

import jax
import jax.numpy as jnp
from jax import lax
from jax.experimental import pallas as pl
from jax.experimental.pallas import tpu as pltpu
from jax.sharding import PartitionSpec as P

REACH = 4
BELOW = REACH - 1
MESH = pl.DeviceIdType.MESH
FIRST = (0, 1, 2, 4)
LAST = (3, 5, 6, 7)
COUNTS = (4, 5, 4)
BASE = (0, 4, 9, 13)
HELD = 13
AHEAD = 5


def dot(a, b):
    return jnp.dot(a, b, preferred_element_type=jnp.float32)


def kernel(
    n, level_ref, cols_ref, right_in, off_in, diag_in, out_ref,
    right_ref, off_ref, diag_ref, turned, in_sem, fac, fac_last, inv, win, land0, land1, land2, sol0, sol1, sol2, sol3, lvl_ref, lvl_in, lvl_s, slot, perm,
    lvl_send, lvl_recv, lvl_sem, x_send, x_recv, c_send, c_recv, f_send, f_recv,
    w0_send, w0_recv, w1_send, w1_recv, w2_send, w2_recv,
):
    rows, kk, part, bs = off_ref.shape
    me, mine = lax.axis_index("rows"), lax.axis_index("rhs")
    core = mine + 1 - 2 * lax.rem(mine, 2)
    across = lax.rem(mine + 2, 4)

    fetches = [
        pltpu.make_async_copy(src, dst, in_sem.at[i])
        for i, (src, dst) in enumerate([(diag_in, diag_ref), (off_in, off_ref), (right_in, right_ref)])
    ]
    for copy in fetches:
        copy.start()
    lvl_in[...] = jnp.zeros_like(lvl_in)
    for r in range(rows):
        lvl_ref[r:r + 1, :] = jnp.full((1, lvl_ref.shape[1]), level_ref[r], jnp.int32)
    barrier = pltpu.get_barrier_semaphore()
    for other in (core, across):
        pl.semaphore_signal(barrier, inc=1, device_id=(me, other), device_id_type=MESH)
    for d in range(1, REACH):
        @pl.when(me + d < n)
        def _():
            pl.semaphore_signal(barrier, inc=1, device_id=(me + d, mine), device_id_type=MESH)

        @pl.when(me >= d)
        def _():
            pl.semaphore_signal(barrier, inc=1, device_id=(me - d, mine), device_id_type=MESH)

    own = [level_ref[r] for r in range(rows)]

    def ranked(levels, base):
        out = []
        lower = jnp.int32(0)
        for r in range(rows):
            lower += (levels[r] < 2).astype(jnp.int32)
        for r in range(rows):
            before = jnp.int32(0)
            for q in range(rows):
                if q < r:
                    before += (levels[q] <= levels[r]).astype(jnp.int32)
                elif q > r:
                    before += (levels[q] < levels[r]).astype(jnp.int32)
            at = jnp.where(levels[r] == 0, before, before - FIRST[1] + BASE[1])
            at = jnp.where(levels[r] == 2, before - lower + BASE[2], at)
            at = jnp.where(levels[r] == 3, before - FIRST[3] + BASE[3], at)
            slot[base * rows + r] = jnp.clip(at + base * HELD, 0, win.shape[0] - 1)
            out.append(before)
        return out, lower

    own_rank, lower2 = ranked(own, BELOW)
    where = []
    for p in range(rows):
        at = jnp.int32(0)
        for r in range(rows):
            at += jnp.where(own_rank[r] == p, r, 0)
        perm[p] = at
        where.append(at)

    def span(who):
        return pl.ds(pl.multiple_of(who * part, part), part)

    def stage_diag(p):
        inv[p, span(mine), :] = diag_ref[where[p]]

    def stage_off(p):
        for k in range(kk):
            if p == rows - 1:
                fac_last[span(mine), k * bs:(k + 1) * bs] = off_ref[where[p], k]
            else:
                fac[p - 1, span(mine), k * bs:(k + 1) * bs] = off_ref[where[p], k]

    half = rows // 2
    early = LAST[1] + 1
    items = [("d", (0, half))] + [("o", p) for p in range(1, half)] + [("d", (half, early))]
    items += [("o", p) for p in range(half, early)] + [("d", (early, rows))] + [("o", p) for p in range(early, rows)]

    def piece(item, who):
        kind, at = item
        if kind == "d":
            return inv.at[at[0]:at[1], span(who), :]
        if at == rows - 1:
            return fac_last.at[span(who), :]
        return fac.at[at - 1, span(who), :]

    def send_x(i):
        return pltpu.make_async_remote_copy(
            piece(items[i], mine), piece(items[i], mine), x_send.at[i], x_recv.at[i],
            device_id=(me, across), device_id_type=MESH)

    def send_c(i):
        return pltpu.make_async_remote_copy(
            piece(items[i], mine), piece(items[i], mine), c_send.at[i], c_recv.at[i],
            device_id=(me, core), device_id_type=MESH)

    def send_f(i):
        return pltpu.make_async_remote_copy(
            piece(items[i], across), piece(items[i], across), f_send.at[i], f_recv.at[i],
            device_id=(me, core), device_id_type=MESH)

    def issue(i):
        if i < len(items):
            send_x(i).start()
            send_c(i).start()

    def arrive(i):
        send_x(i).wait_recv()
        send_f(i).start()
        send_x(i).wait_send()
        issue(i + AHEAD)
        send_c(i).wait_recv()
        send_f(i).wait_recv()

    fetches[0].wait()
    for p in range(rows):
        stage_diag(p)

    greeted = jnp.int32(2)
    for d in range(1, REACH):
        greeted += (me + d < n).astype(jnp.int32) + (me >= d).astype(jnp.int32)
    pl.semaphore_wait(barrier, greeted)

    issue(0)
    fetches[1].wait()
    staged = 0
    for i in range(1, AHEAD):
        kind, at = items[i]
        if kind == "o":
            stage_off(at)
            staged = at
        issue(i)
    for p in range(staged + 1, rows):
        stage_off(p)
    fetches[2].wait()
    for r in range(rows):
        turned[r] = right_ref[r].astype(jnp.float32).T

    def send_lvl(d):
        return pltpu.make_async_remote_copy(
            lvl_ref, lvl_in.at[BELOW - d], lvl_send.at[d - 1], lvl_recv.at[d - 1],
            device_id=(me + d, mine), device_id_type=MESH)

    def each_up(what):
        for d in range(1, REACH):
            @pl.when(me + d < n)
            def _():
                what(d)

    def each_down(what):
        for d in range(1, REACH):
            @pl.when(me >= d)
            def _():
                what(d)

    even = lax.rem(me, 2) == 0
    odd = lax.rem(me, 2) == 1
    sols, lands = (sol0, sol1, sol2), (land0, land1, land2)
    hop_send, hop_recv = (w0_send, w1_send, w2_send), (w0_recv, w1_recv, w2_recv)
    OWN_UP, OWN_SIDE, PASS_SIDE, PASS_UP = range(4)

    def hop(v, i, way, to, d):
        src = sols[v].at[i]
        if way == PASS_SIDE:
            src = lands[v].at[BELOW - 2, i]
        if way == PASS_UP:
            src = lands[v].at[BELOW - 1, i]
        return pltpu.make_async_remote_copy(
            src, lands[v].at[BELOW - d, i], hop_send[v].at[i, way], hop_recv[v].at[i, d - 1],
            device_id=(to, mine), device_id_type=MESH)

    def landed(v, i, d):
        hop(v, i, OWN_UP, me, d).wait_recv()

    def own_hops(v, i, what):
        @pl.when(me + 2 < n)
        def _():
            what(hop(v, i, OWN_UP, me + 2, 2))

        @pl.when(even)
        def _():
            what(hop(v, i, OWN_SIDE, me + 1, 1))

    def side_hops(v, i, what):
        @pl.when(even & (me >= 2))
        def _():
            what(hop(v, i, PASS_SIDE, me + 1, 3))

        @pl.when(odd & (me >= 2))
        def _():
            what(hop(v, i, PASS_SIDE, me - 1, 1))

    def up_hops(v, i, what):
        @pl.when(even & (me >= 2) & (me + 2 < n))
        def _():
            what(hop(v, i, PASS_UP, me + 2, 3))

    def start(copy):
        copy.start()

    def first_leg(v, i):
        @pl.when(me >= 2)
        def _():
            landed(v, i, 2)
        side_hops(v, i, start)

    def second_leg(v, i):
        @pl.when(me >= 1)
        def _():
            landed(v, i, 1)
        up_hops(v, i, start)

    def third_leg(v, i):
        @pl.when(me >= 3)
        def _():
            landed(v, i, 3)

    def serve(v, i):
        count = sols[v].shape[0]
        for leg, late in ((first_leg, 1), (second_leg, 2), (third_leg, 3)):
            if 0 <= i - late < count:
                leg(v, i - late)

    def serve_rest(v):
        count = sols[v].shape[0]
        for i in range(count, count + 3):
            serve(v, i)

    each_up(lambda d: send_lvl(d).start())

    at_item = {p: items.index(("o", p)) for p in range(1, rows)}
    arrive(0)
    for p in range(half):
        sol0[p] = dot(inv[p], turned[where[p]].astype(jnp.bfloat16)).astype(jnp.bfloat16)
        own_hops(0, p, start)

    each_down(lambda d: send_lvl(d).wait_recv())
    fetch = pltpu.make_async_copy(lvl_in, lvl_s, lvl_sem)
    fetch.start()
    fetch.wait()
    for o in range(BELOW):
        ranked([lvl_s[o, r, 0] for r in range(rows)], o)

    def solve(p, factor, inverse):
        row = perm[p]
        taken = []
        for k in range(kk):
            at = cols_ref[row, k] - (me - BELOW) * rows
            taken.append(win[slot[jnp.clip(at, 0, REACH * rows - 1)]])
        contribution = dot(factor, jnp.concatenate(taken, axis=0))
        residue = (turned[row] - contribution).astype(jnp.bfloat16)
        return dot(inverse, residue).astype(jnp.bfloat16)

    def fill(v):
        for d in range(1, REACH):
            o = (BELOW - d) * HELD + BASE[v]
            win[o:o + COUNTS[v]] = lands[v][BELOW - d]
        o = BELOW * HELD + BASE[v]
        win[o:o + COUNTS[v]] = sols[v][...]

    arrive(at_item[1])
    for i in range(half):
        serve(0, i)
    arrive(at_item[2])
    serve_rest(0)
    fill(0)

    for p in range(FIRST[1], LAST[1] + 1):
        if p == half:
            arrive(items.index(("d", (half, early))))
        if p > 2:
            arrive(at_item[p])
        i = p - FIRST[1]
        sol1[i] = solve(p, fac[p - 1], inv[p])
        own_hops(1, i, start)
        serve(1, i)
    serve_rest(1)
    fill(1)

    arrive(items.index(("d", (early, rows))))
    for p in range(early, rows - 1):
        arrive(at_item[p])
    for i in range(COUNTS[2]):
        p = jnp.clip(lower2 + i, FIRST[2], LAST[2])
        sol2[i] = solve(p, fac[p - 1], inv[p])
        own_hops(2, i, start)
        serve(2, i)
    arrive(at_item[rows - 1])
    serve_rest(2)
    fill(2)

    for p in range(FIRST[3], rows):
        sol3[p - FIRST[3]] = solve(p, fac_last[...] if p == rows - 1 else fac[p - 1], inv[p])
    win[BELOW * HELD + BASE[3]:] = sol3[...]
    for r in range(rows):
        out_ref[r] = win[slot[BELOW * rows + r]]

    for i in range(len(items)):
        send_c(i).wait_send()
        send_f(i).wait_send()

    each_up(lambda d: send_lvl(d).wait_send())
    for v in range(BELOW):
        for i in range(sols[v].shape[0]):
            for hops in (own_hops, side_hops, up_hops):
                hops(v, i, lambda copy: copy.wait_send())


def per_device(n, right_side, off_blocks, diag_inverse, block_level, block_columns):
    rows, kk, part, bs = off_blocks.shape
    samples = right_side.shape[1]
    vmem = pl.BlockSpec(memory_space=pltpu.VMEM)
    smem = pl.BlockSpec(memory_space=pltpu.SMEM)
    anywhere = pl.BlockSpec(memory_space=pltpu.HBM)
    tile = (bs, samples)
    counts = COUNTS
    items = rows + 2
    dma = pltpu.SemaphoreType.DMA
    answer = pl.pallas_call(
        functools.partial(kernel, n),
        out_shape=jax.ShapeDtypeStruct((rows,) + tile, jnp.bfloat16),
        in_specs=[smem, smem, anywhere, anywhere, anywhere],
        out_specs=vmem,
        scratch_shapes=[
            pltpu.VMEM(right_side.shape, jnp.bfloat16),
            pltpu.VMEM(off_blocks.shape, jnp.bfloat16),
            pltpu.VMEM(diag_inverse.shape, jnp.bfloat16),
            pltpu.VMEM((rows,) + tile, jnp.float32),
            dma((3,)),
            pltpu.VMEM((rows - 2, 4 * part, kk * bs), jnp.bfloat16),
            pltpu.VMEM((4 * part, kk * bs), jnp.bfloat16),
            pltpu.VMEM((rows, 4 * part, bs), jnp.bfloat16),
            pltpu.VMEM((REACH * HELD + rows - FIRST[3],) + tile, jnp.bfloat16),
            pltpu.VMEM((BELOW, counts[0]) + tile, jnp.bfloat16),
            pltpu.VMEM((BELOW, counts[1]) + tile, jnp.bfloat16),
            pltpu.VMEM((BELOW, counts[2]) + tile, jnp.bfloat16),
            pltpu.VMEM((counts[0],) + tile, jnp.bfloat16),
            pltpu.VMEM((counts[1],) + tile, jnp.bfloat16),
            pltpu.VMEM((counts[2],) + tile, jnp.bfloat16),
            pltpu.VMEM((rows - FIRST[3],) + tile, jnp.bfloat16),
            pltpu.VMEM((rows, 128), jnp.int32),
            pltpu.VMEM((BELOW, rows, 128), jnp.int32),
            pltpu.SMEM((BELOW, rows, 128), jnp.int32),
            pltpu.SMEM((REACH * rows,), jnp.int32),
            pltpu.SMEM((rows,), jnp.int32),
            dma((BELOW,)), dma((BELOW,)), dma,
            dma((items,)), dma((items,)), dma((items,)), dma((items,)), dma((items,)), dma((items,)),
            dma((counts[0], 4)), dma((counts[0], BELOW)),
            dma((counts[1], 4)), dma((counts[1], BELOW)),
            dma((counts[2], 4)), dma((counts[2], BELOW)),
        ],
        compiler_params=pltpu.CompilerParams(
            collective_id=0, has_side_effects=True, vmem_limit_bytes=62 * 2 ** 20),
    )(
        block_level, block_columns, right_side, off_blocks, diag_inverse,
    )
    return jnp.swapaxes(answer, 1, 2)


def solution(mesh):
    return jax.shard_map(
        functools.partial(per_device, mesh.shape["rows"]),
        mesh=mesh,
        in_specs=(
            P("rows", "rhs", None),
            P("rows", None, "rhs", None),
            P("rows", "rhs", None),
            P("rows"),
            P("rows", None),
        ),
        out_specs=P("rows", "rhs", None),
        check_vma=False,
    )
```

```python
import functools

import jax
import jax.numpy as jnp
from jax import lax
from jax.experimental import pallas as pl
from jax.experimental.pallas import tpu as pltpu
from jax.sharding import PartitionSpec as P

REACH = 4
BELOW = REACH - 1
MESH = pl.DeviceIdType.MESH
FIRST = (0, 1, 2, 4)
LAST = (3, 5, 6, 7)
COUNTS = (4, 5, 4)
BASE = (0, 4, 9, 13)
HELD = 13
AHEAD = 5
SPLIT = 2


def dot(a, b):
    return jnp.dot(a, b, preferred_element_type=jnp.float32)


def kernel(
    n, level_ref, cols_ref, right_in, off_in, diag_in, out_ref,
    right_ref, off_ref, diag_ref, turned, in_sem, fac, fac_last, inv, win, land0, land1, land2, sol0, sol1, sol2, sol3, lvl_ref, lvl_in, lvl_s, slot, perm,
    lvl_send, lvl_recv, lvl_sem, x_send, x_recv, c_send, c_recv, f_send, f_recv,
    w0_send, w0_recv, w1_send, w1_recv, w2_send, w2_recv,
):
    rows, kk, part, bs = off_ref.shape
    me, mine = lax.axis_index("rows"), lax.axis_index("rhs")
    core = mine + 1 - 2 * lax.rem(mine, 2)
    across = lax.rem(mine + 2, 4)

    fetches = [
        pltpu.make_async_copy(src, dst, in_sem.at[i])
        for i, (src, dst) in enumerate([(diag_in, diag_ref), (off_in, off_ref), (right_in, right_ref)])
    ]
    for copy in fetches:
        copy.start()
    lvl_in[...] = jnp.zeros_like(lvl_in)
    for r in range(rows):
        lvl_ref[r:r + 1, :] = jnp.full((1, lvl_ref.shape[1]), level_ref[r], jnp.int32)
    barrier = pltpu.get_barrier_semaphore()
    for other in (core, across):
        pl.semaphore_signal(barrier, inc=1, device_id=(me, other), device_id_type=MESH)
    for d in range(1, REACH):
        @pl.when(me + d < n)
        def _():
            pl.semaphore_signal(barrier, inc=1, device_id=(me + d, mine), device_id_type=MESH)

        @pl.when(me >= d)
        def _():
            pl.semaphore_signal(barrier, inc=1, device_id=(me - d, mine), device_id_type=MESH)

    own = [level_ref[r] for r in range(rows)]

    def ranked(levels, base):
        out = []
        lower = jnp.int32(0)
        for r in range(rows):
            lower += (levels[r] < 2).astype(jnp.int32)
        for r in range(rows):
            before = jnp.int32(0)
            for q in range(rows):
                if q < r:
                    before += (levels[q] <= levels[r]).astype(jnp.int32)
                elif q > r:
                    before += (levels[q] < levels[r]).astype(jnp.int32)
            at = jnp.where(levels[r] == 0, before, before - FIRST[1] + BASE[1])
            at = jnp.where(levels[r] == 2, before - lower + BASE[2], at)
            at = jnp.where(levels[r] == 3, before - FIRST[3] + BASE[3], at)
            slot[base * rows + r] = jnp.clip(at + base * HELD, 0, win.shape[0] - 1)
            out.append(before)
        return out, lower

    own_rank, lower2 = ranked(own, BELOW)
    where = []
    for p in range(rows):
        at = jnp.int32(0)
        for r in range(rows):
            at += jnp.where(own_rank[r] == p, r, 0)
        perm[p] = at
        where.append(at)

    def span(who):
        return pl.ds(pl.multiple_of(who * part, part), part)

    def stage_diag(p):
        inv[p, span(mine), :] = diag_ref[where[p]]

    def stage_off(p):
        for k in range(kk):
            if p == rows - 1:
                fac_last[span(mine), k * bs:(k + 1) * bs] = off_ref[where[p], k]
            else:
                fac[p - 1, span(mine), k * bs:(k + 1) * bs] = off_ref[where[p], k]

    half = rows // 2
    early = LAST[1] + 1
    items = [("d", (0, half))] + [("o", p) for p in range(1, half)] + [("d", (half, early))]
    items += [("o", p) for p in range(half, early)] + [("d", (early, rows))] + [("o", p) for p in range(early, rows)]

    def piece(item, who):
        kind, at = item
        if kind == "d":
            return inv.at[at[0]:at[1], span(who), :]
        if at == rows - 1:
            return fac_last.at[span(who), :]
        return fac.at[at - 1, span(who), :]

    def send_x(i):
        return pltpu.make_async_remote_copy(
            piece(items[i], mine), piece(items[i], mine), x_send.at[i], x_recv.at[i],
            device_id=(me, across), device_id_type=MESH)

    def send_c(i):
        return pltpu.make_async_remote_copy(
            piece(items[i], mine), piece(items[i], mine), c_send.at[i], c_recv.at[i],
            device_id=(me, core), device_id_type=MESH)

    def send_f(i):
        return pltpu.make_async_remote_copy(
            piece(items[i], across), piece(items[i], across), f_send.at[i], f_recv.at[i],
            device_id=(me, core), device_id_type=MESH)

    def issue(i):
        if i < len(items):
            send_x(i).start()
            send_c(i).start()

    def arrive(i):
        send_x(i).wait_recv()
        send_f(i).start()
        send_x(i).wait_send()
        issue(i + AHEAD)
        send_c(i).wait_recv()
        send_f(i).wait_recv()

    fetches[0].wait()
    for p in range(rows):
        stage_diag(p)

    greeted = jnp.int32(2)
    for d in range(1, REACH):
        greeted += (me + d < n).astype(jnp.int32) + (me >= d).astype(jnp.int32)
    pl.semaphore_wait(barrier, greeted)

    issue(0)
    fetches[1].wait()
    staged = 0
    for i in range(1, AHEAD):
        kind, at = items[i]
        if kind == "o":
            stage_off(at)
            staged = at
        issue(i)
    for p in range(staged + 1, rows):
        stage_off(p)
    fetches[2].wait()
    for r in range(rows):
        turned[r] = right_ref[r].astype(jnp.float32).T

    def send_lvl(d):
        return pltpu.make_async_remote_copy(
            lvl_ref, lvl_in.at[BELOW - d], lvl_send.at[d - 1], lvl_recv.at[d - 1],
            device_id=(me + d, mine), device_id_type=MESH)

    def each_up(what):
        for d in range(1, REACH):
            @pl.when(me + d < n)
            def _():
                what(d)

    def each_down(what):
        for d in range(1, REACH):
            @pl.when(me >= d)
            def _():
                what(d)

    even = lax.rem(me, 2) == 0
    odd = lax.rem(me, 2) == 1
    sols, lands = (sol0, sol1, sol2), (land0, land1, land2)
    hop_send, hop_recv = (w0_send, w1_send, w2_send), (w0_recv, w1_recv, w2_recv)
    OWN_UP, OWN_SIDE, PASS_SIDE, PASS_UP = range(4)

    def hop(v, i, way, to, d):
        src = sols[v].at[i]
        if way == PASS_SIDE:
            src = lands[v].at[BELOW - 2, i]
        if way == PASS_UP:
            src = lands[v].at[BELOW - 1, i]
        return pltpu.make_async_remote_copy(
            src, lands[v].at[BELOW - d, i], hop_send[v].at[i, way], hop_recv[v].at[i, d - 1],
            device_id=(to, mine), device_id_type=MESH)

    def landed(v, i, d):
        hop(v, i, OWN_UP, me, d).wait_recv()

    def own_hops(v, i, what):
        @pl.when(me + 2 < n)
        def _():
            what(hop(v, i, OWN_UP, me + 2, 2))

        @pl.when(even)
        def _():
            what(hop(v, i, OWN_SIDE, me + 1, 1))

    def side_hops(v, i, what):
        @pl.when(even & (me >= 2))
        def _():
            what(hop(v, i, PASS_SIDE, me + 1, 3))

        @pl.when(odd & (me >= 2))
        def _():
            what(hop(v, i, PASS_SIDE, me - 1, 1))

    def up_hops(v, i, what):
        @pl.when(even & (me >= 2) & (me + 2 < n))
        def _():
            what(hop(v, i, PASS_UP, me + 2, 3))

    def start(copy):
        copy.start()

    def first_leg(v, i):
        @pl.when(me >= 2)
        def _():
            landed(v, i, 2)
        side_hops(v, i, start)

    def second_leg(v, i):
        @pl.when(me >= 1)
        def _():
            landed(v, i, 1)
        up_hops(v, i, start)

    def third_leg(v, i):
        @pl.when(me >= 3)
        def _():
            landed(v, i, 3)

    def legs(leg, v, first, last):
        for i in range(SPLIT * max(first, 0), SPLIT * max(last, 0)):
            leg(v, i)

    def serve(v, i):
        legs(first_leg, v, i - 1, i)
        legs(second_leg, v, i - 2, i - 1)
        legs(third_leg, v, i - 3, i - 2)

    def serve_rest(v):
        count = COUNTS[v]
        legs(second_leg, v, count - 2, count - 1)
        legs(first_leg, v, count - 1, count)
        legs(second_leg, v, count - 1, count)
        legs(third_leg, v, count - 3, count)

    def serve_all(v, between=None):
        count = SPLIT * COUNTS[v]
        for i in range(count + SPLIT):
            if i < count:
                first_leg(v, i)
            if i >= SPLIT:
                second_leg(v, i - SPLIT)
        if between is not None:
            between()
        legs(third_leg, v, 0, COUNTS[v])

    def put(v, i, block):
        sols[v][SPLIT * i:SPLIT * (i + 1)] = block.reshape((SPLIT,) + sols[v].shape[1:])
        for j in range(SPLIT * i, SPLIT * (i + 1)):
            own_hops(v, j, start)

    each_up(lambda d: send_lvl(d).start())

    at_item = {p: items.index(("o", p)) for p in range(1, rows)}
    arrive(0)
    for p in range(half):
        put(0, p, dot(inv[p], turned[where[p]].astype(jnp.bfloat16)).astype(jnp.bfloat16))

    each_down(lambda d: send_lvl(d).wait_recv())
    fetch = pltpu.make_async_copy(lvl_in, lvl_s, lvl_sem)
    fetch.start()
    fetch.wait()
    for o in range(BELOW):
        ranked([lvl_s[o, r, 0] for r in range(rows)], o)

    def solve(p, factor, inverse):
        row = perm[p]
        taken = []
        for k in range(kk):
            at = cols_ref[row, k] - (me - BELOW) * rows
            taken.append(win[slot[jnp.clip(at, 0, REACH * rows - 1)]])
        contribution = dot(factor, jnp.concatenate(taken, axis=0))
        residue = (turned[row] - contribution).astype(jnp.bfloat16)
        return dot(inverse, residue).astype(jnp.bfloat16)

    def fill(v):
        for d in range(1, REACH):
            o = (BELOW - d) * HELD + BASE[v]
            win[o:o + COUNTS[v]] = lands[v][BELOW - d].reshape((COUNTS[v],) + win.shape[1:])
        o = BELOW * HELD + BASE[v]
        win[o:o + COUNTS[v]] = sols[v][...].reshape((COUNTS[v],) + win.shape[1:])

    arrive(at_item[1])
    serve_all(0, lambda: arrive(at_item[2]))
    fill(0)

    for p in range(FIRST[1], LAST[1] + 1):
        if p == half:
            arrive(items.index(("d", (half, early))))
        if p > 2:
            arrive(at_item[p])
        i = p - FIRST[1]
        put(1, i, solve(p, fac[p - 1], inv[p]))
        serve(1, i)
    serve_rest(1)
    fill(1)

    arrive(items.index(("d", (early, rows))))
    for p in range(early, rows - 1):
        arrive(at_item[p])
    for i in range(COUNTS[2]):
        p = jnp.clip(lower2 + i, FIRST[2], LAST[2])
        put(2, i, solve(p, fac[p - 1], inv[p]))
    serve_all(2, lambda: arrive(at_item[rows - 1]))
    fill(2)

    for p in range(FIRST[3], rows):
        sol3[p - FIRST[3]] = solve(p, fac_last[...] if p == rows - 1 else fac[p - 1], inv[p])
    win[BELOW * HELD + BASE[3]:] = sol3[...]
    for r in range(rows):
        out_ref[r] = win[slot[BELOW * rows + r]]

    for i in range(len(items)):
        send_c(i).wait_send()
        send_f(i).wait_send()

    each_up(lambda d: send_lvl(d).wait_send())
    for v in range(BELOW):
        for i in range(SPLIT * COUNTS[v]):
            for hops in (own_hops, side_hops, up_hops):
                hops(v, i, lambda copy: copy.wait_send())


def per_device(n, right_side, off_blocks, diag_inverse, block_level, block_columns):
    rows, kk, part, bs = off_blocks.shape
    samples = right_side.shape[1]
    vmem = pl.BlockSpec(memory_space=pltpu.VMEM)
    smem = pl.BlockSpec(memory_space=pltpu.SMEM)
    anywhere = pl.BlockSpec(memory_space=pltpu.HBM)
    tile = (bs, samples)
    sent = (bs // SPLIT, samples)
    counts = [SPLIT * count for count in COUNTS]
    items = rows + 2
    dma = pltpu.SemaphoreType.DMA
    answer = pl.pallas_call(
        functools.partial(kernel, n),
        out_shape=jax.ShapeDtypeStruct((rows,) + tile, jnp.bfloat16),
        in_specs=[smem, smem, anywhere, anywhere, anywhere],
        out_specs=vmem,
        scratch_shapes=[
            pltpu.VMEM(right_side.shape, jnp.bfloat16),
            pltpu.VMEM(off_blocks.shape, jnp.bfloat16),
            pltpu.VMEM(diag_inverse.shape, jnp.bfloat16),
            pltpu.VMEM((rows,) + tile, jnp.float32),
            dma((3,)),
            pltpu.VMEM((rows - 2, 4 * part, kk * bs), jnp.bfloat16),
            pltpu.VMEM((4 * part, kk * bs), jnp.bfloat16),
            pltpu.VMEM((rows, 4 * part, bs), jnp.bfloat16),
            pltpu.VMEM((REACH * HELD + rows - FIRST[3],) + tile, jnp.bfloat16),
            pltpu.VMEM((BELOW, counts[0]) + sent, jnp.bfloat16),
            pltpu.VMEM((BELOW, counts[1]) + sent, jnp.bfloat16),
            pltpu.VMEM((BELOW, counts[2]) + sent, jnp.bfloat16),
            pltpu.VMEM((counts[0],) + sent, jnp.bfloat16),
            pltpu.VMEM((counts[1],) + sent, jnp.bfloat16),
            pltpu.VMEM((counts[2],) + sent, jnp.bfloat16),
            pltpu.VMEM((rows - FIRST[3],) + tile, jnp.bfloat16),
            pltpu.VMEM((rows, 128), jnp.int32),
            pltpu.VMEM((BELOW, rows, 128), jnp.int32),
            pltpu.SMEM((BELOW, rows, 128), jnp.int32),
            pltpu.SMEM((REACH * rows,), jnp.int32),
            pltpu.SMEM((rows,), jnp.int32),
            dma((BELOW,)), dma((BELOW,)), dma,
            dma((items,)), dma((items,)), dma((items,)), dma((items,)), dma((items,)), dma((items,)),
            dma((counts[0], 4)), dma((counts[0], BELOW)),
            dma((counts[1], 4)), dma((counts[1], BELOW)),
            dma((counts[2], 4)), dma((counts[2], BELOW)),
        ],
        compiler_params=pltpu.CompilerParams(
            collective_id=0, has_side_effects=True, vmem_limit_bytes=62 * 2 ** 20),
    )(
        block_level, block_columns, right_side, off_blocks, diag_inverse,
    )
    return jnp.swapaxes(answer, 1, 2)


def solution(mesh):
    return jax.shard_map(
        functools.partial(per_device, mesh.shape["rows"]),
        mesh=mesh,
        in_specs=(
            P("rows", "rhs", None),
            P("rows", None, "rhs", None),
            P("rows", "rhs", None),
            P("rows"),
            P("rows", None),
        ),
        out_specs=P("rows", "rhs", None),
        check_vma=False,
    )
```

```python
import functools

import jax
import jax.numpy as jnp
from jax import lax
from jax.experimental import pallas as pl
from jax.experimental.pallas import tpu as pltpu
from jax.sharding import PartitionSpec as P

REACH = 4
BELOW = REACH - 1
MESH = pl.DeviceIdType.MESH
FIRST = (0, 1, 2, 4)
LAST = (3, 5, 6, 7)
COUNTS = (4, 5, 4)
BASE = (0, 4, 9, 13)
HELD = 13
AHEAD = 5
SPLIT = 4


def dot(a, b):
    return jnp.dot(a, b, preferred_element_type=jnp.float32)


def kernel(
    n, level_ref, cols_ref, right_in, off_in, diag_in, out_ref,
    right_ref, off_ref, diag_ref, turned, in_sem, fac, fac_last, inv, win, land0, land1, land2, sol0, sol1, sol2, sol3, lvl_ref, lvl_in, lvl_s, slot, perm,
    lvl_send, lvl_recv, lvl_sem, x_send, x_recv, c_send, c_recv, f_send, f_recv,
    w0_send, w0_recv, w1_send, w1_recv, w2_send, w2_recv,
):
    rows, kk, part, bs = off_ref.shape
    me, mine = lax.axis_index("rows"), lax.axis_index("rhs")
    core = mine + 1 - 2 * lax.rem(mine, 2)
    across = lax.rem(mine + 2, 4)

    fetches = [
        pltpu.make_async_copy(src, dst, in_sem.at[i])
        for i, (src, dst) in enumerate([(diag_in, diag_ref), (off_in, off_ref), (right_in, right_ref)])
    ]
    for copy in fetches:
        copy.start()
    lvl_in[...] = jnp.zeros_like(lvl_in)
    for r in range(rows):
        lvl_ref[r:r + 1, :] = jnp.full((1, lvl_ref.shape[1]), level_ref[r], jnp.int32)
    barrier = pltpu.get_barrier_semaphore()
    for other in (core, across):
        pl.semaphore_signal(barrier, inc=1, device_id=(me, other), device_id_type=MESH)
    for d in range(1, REACH):
        @pl.when(me + d < n)
        def _():
            pl.semaphore_signal(barrier, inc=1, device_id=(me + d, mine), device_id_type=MESH)

        @pl.when(me >= d)
        def _():
            pl.semaphore_signal(barrier, inc=1, device_id=(me - d, mine), device_id_type=MESH)

    own = [level_ref[r] for r in range(rows)]

    def ranked(levels, base):
        out = []
        lower = jnp.int32(0)
        for r in range(rows):
            lower += (levels[r] < 2).astype(jnp.int32)
        for r in range(rows):
            before = jnp.int32(0)
            for q in range(rows):
                if q < r:
                    before += (levels[q] <= levels[r]).astype(jnp.int32)
                elif q > r:
                    before += (levels[q] < levels[r]).astype(jnp.int32)
            at = jnp.where(levels[r] == 0, before, before - FIRST[1] + BASE[1])
            at = jnp.where(levels[r] == 2, before - lower + BASE[2], at)
            at = jnp.where(levels[r] == 3, before - FIRST[3] + BASE[3], at)
            slot[base * rows + r] = jnp.clip(at + base * HELD, 0, win.shape[0] - 1)
            out.append(before)
        return out, lower

    own_rank, lower2 = ranked(own, BELOW)
    where = []
    for p in range(rows):
        at = jnp.int32(0)
        for r in range(rows):
            at += jnp.where(own_rank[r] == p, r, 0)
        perm[p] = at
        where.append(at)

    def span(who):
        return pl.ds(pl.multiple_of(who * part, part), part)

    def stage_diag(p):
        inv[p, span(mine), :] = diag_ref[where[p]]

    def stage_off(p):
        for k in range(kk):
            if p == rows - 1:
                fac_last[span(mine), k * bs:(k + 1) * bs] = off_ref[where[p], k]
            else:
                fac[p - 1, span(mine), k * bs:(k + 1) * bs] = off_ref[where[p], k]

    half = rows // 2
    early = LAST[1] + 1
    items = [("d", (0, half))] + [("o", p) for p in range(1, half)] + [("d", (half, early))]
    items += [("o", p) for p in range(half, early)] + [("d", (early, rows))] + [("o", p) for p in range(early, rows)]

    def piece(item, who):
        kind, at = item
        if kind == "d":
            return inv.at[at[0]:at[1], span(who), :]
        if at == rows - 1:
            return fac_last.at[span(who), :]
        return fac.at[at - 1, span(who), :]

    def send_x(i):
        return pltpu.make_async_remote_copy(
            piece(items[i], mine), piece(items[i], mine), x_send.at[i], x_recv.at[i],
            device_id=(me, across), device_id_type=MESH)

    def send_c(i):
        return pltpu.make_async_remote_copy(
            piece(items[i], mine), piece(items[i], mine), c_send.at[i], c_recv.at[i],
            device_id=(me, core), device_id_type=MESH)

    def send_f(i):
        return pltpu.make_async_remote_copy(
            piece(items[i], across), piece(items[i], across), f_send.at[i], f_recv.at[i],
            device_id=(me, core), device_id_type=MESH)

    def issue(i):
        if i < len(items):
            send_x(i).start()
            send_c(i).start()

    def arrive(i):
        send_x(i).wait_recv()
        send_f(i).start()
        send_x(i).wait_send()
        issue(i + AHEAD)
        send_c(i).wait_recv()
        send_f(i).wait_recv()

    fetches[0].wait()
    for p in range(rows):
        stage_diag(p)

    greeted = jnp.int32(2)
    for d in range(1, REACH):
        greeted += (me + d < n).astype(jnp.int32) + (me >= d).astype(jnp.int32)
    pl.semaphore_wait(barrier, greeted)

    issue(0)
    fetches[1].wait()
    staged = 0
    for i in range(1, AHEAD):
        kind, at = items[i]
        if kind == "o":
            stage_off(at)
            staged = at
        issue(i)
    for p in range(staged + 1, rows):
        stage_off(p)
    fetches[2].wait()
    for r in range(rows):
        turned[r] = right_ref[r].astype(jnp.float32).T

    def send_lvl(d):
        return pltpu.make_async_remote_copy(
            lvl_ref, lvl_in.at[BELOW - d], lvl_send.at[d - 1], lvl_recv.at[d - 1],
            device_id=(me + d, mine), device_id_type=MESH)

    def each_up(what):
        for d in range(1, REACH):
            @pl.when(me + d < n)
            def _():
                what(d)

    def each_down(what):
        for d in range(1, REACH):
            @pl.when(me >= d)
            def _():
                what(d)

    even = lax.rem(me, 2) == 0
    odd = lax.rem(me, 2) == 1
    sols, lands = (sol0, sol1, sol2), (land0, land1, land2)
    hop_send, hop_recv = (w0_send, w1_send, w2_send), (w0_recv, w1_recv, w2_recv)
    OWN_UP, OWN_SIDE, PASS_SIDE, PASS_UP = range(4)

    def hop(v, i, way, to, d):
        src = sols[v].at[i]
        if way == PASS_SIDE:
            src = lands[v].at[BELOW - 2, i]
        if way == PASS_UP:
            src = lands[v].at[BELOW - 1, i]
        return pltpu.make_async_remote_copy(
            src, lands[v].at[BELOW - d, i], hop_send[v].at[i, way], hop_recv[v].at[i, d - 1],
            device_id=(to, mine), device_id_type=MESH)

    def landed(v, i, d):
        hop(v, i, OWN_UP, me, d).wait_recv()

    def own_hops(v, i, what):
        @pl.when(me + 2 < n)
        def _():
            what(hop(v, i, OWN_UP, me + 2, 2))

        @pl.when(even)
        def _():
            what(hop(v, i, OWN_SIDE, me + 1, 1))

    def side_hops(v, i, what):
        if i % 2 == 0:
            @pl.when(even & (me >= 2))
            def _():
                what(hop(v, i, PASS_SIDE, me + 1, 3))

        @pl.when(odd & (me >= 2))
        def _():
            what(hop(v, i, PASS_SIDE, me - 1, 1))

    def up_hops(v, i, what):
        passes = even & (me >= 2) if i % 2 == 0 else me >= 1

        @pl.when(passes & (me + 2 < n))
        def _():
            what(hop(v, i, PASS_UP, me + 2, 3))

    def start(copy):
        copy.start()

    def first_leg(v, i):
        @pl.when(me >= 2)
        def _():
            landed(v, i, 2)
        side_hops(v, i, start)

    def second_leg(v, i):
        @pl.when(me >= 1)
        def _():
            landed(v, i, 1)
        up_hops(v, i, start)

    def third_leg(v, i):
        @pl.when(me >= 3)
        def _():
            landed(v, i, 3)

    def legs(leg, v, first, last):
        for i in range(SPLIT * max(first, 0), SPLIT * max(last, 0)):
            leg(v, i)

    def serve(v, i):
        legs(first_leg, v, i - 1, i)
        legs(second_leg, v, i - 2, i - 1)
        legs(third_leg, v, i - 3, i - 2)

    def serve_rest(v):
        count = COUNTS[v]
        legs(second_leg, v, count - 2, count - 1)
        legs(first_leg, v, count - 1, count)
        legs(second_leg, v, count - 1, count)
        legs(third_leg, v, count - 3, count)

    def serve_all(v, between=None):
        count = SPLIT * COUNTS[v]
        for i in range(count + SPLIT):
            if i < count:
                first_leg(v, i)
            if i >= SPLIT:
                second_leg(v, i - SPLIT)
        if between is not None:
            between()
        legs(third_leg, v, 0, COUNTS[v])

    def put(v, i, block):
        sols[v][SPLIT * i:SPLIT * (i + 1)] = block.reshape((SPLIT,) + sols[v].shape[1:])
        for j in range(SPLIT * i, SPLIT * (i + 1)):
            own_hops(v, j, start)

    each_up(lambda d: send_lvl(d).start())

    at_item = {p: items.index(("o", p)) for p in range(1, rows)}
    arrive(0)
    for p in range(half):
        put(0, p, dot(inv[p], turned[where[p]].astype(jnp.bfloat16)).astype(jnp.bfloat16))

    each_down(lambda d: send_lvl(d).wait_recv())
    fetch = pltpu.make_async_copy(lvl_in, lvl_s, lvl_sem)
    fetch.start()
    fetch.wait()
    for o in range(BELOW):
        ranked([lvl_s[o, r, 0] for r in range(rows)], o)

    def solve(p, factor, inverse):
        row = perm[p]
        taken = []
        for k in range(kk):
            at = cols_ref[row, k] - (me - BELOW) * rows
            taken.append(win[slot[jnp.clip(at, 0, REACH * rows - 1)]])
        contribution = dot(factor, jnp.concatenate(taken, axis=0))
        residue = (turned[row] - contribution).astype(jnp.bfloat16)
        return dot(inverse, residue).astype(jnp.bfloat16)

    def fill(v):
        for d in range(1, REACH):
            o = (BELOW - d) * HELD + BASE[v]
            win[o:o + COUNTS[v]] = lands[v][BELOW - d].reshape((COUNTS[v],) + win.shape[1:])
        o = BELOW * HELD + BASE[v]
        win[o:o + COUNTS[v]] = sols[v][...].reshape((COUNTS[v],) + win.shape[1:])

    arrive(at_item[1])
    serve_all(0, lambda: arrive(at_item[2]))
    fill(0)

    for p in range(FIRST[1], LAST[1] + 1):
        if p == half:
            arrive(items.index(("d", (half, early))))
        if p > 2:
            arrive(at_item[p])
        i = p - FIRST[1]
        put(1, i, solve(p, fac[p - 1], inv[p]))
        serve(1, i)
    serve_rest(1)
    fill(1)

    arrive(items.index(("d", (early, rows))))
    for p in range(early, rows - 1):
        arrive(at_item[p])
    for i in range(COUNTS[2]):
        p = jnp.clip(lower2 + i, FIRST[2], LAST[2])
        put(2, i, solve(p, fac[p - 1], inv[p]))
    serve_all(2, lambda: arrive(at_item[rows - 1]))
    fill(2)

    for p in range(FIRST[3], rows):
        sol3[p - FIRST[3]] = solve(p, fac_last[...] if p == rows - 1 else fac[p - 1], inv[p])
    win[BELOW * HELD + BASE[3]:] = sol3[...]
    for r in range(rows):
        out_ref[r] = win[slot[BELOW * rows + r]]

    for i in range(len(items)):
        send_c(i).wait_send()
        send_f(i).wait_send()

    each_up(lambda d: send_lvl(d).wait_send())
    for v in range(BELOW):
        for i in range(SPLIT * COUNTS[v]):
            for hops in (own_hops, side_hops, up_hops):
                hops(v, i, lambda copy: copy.wait_send())


def per_device(n, right_side, off_blocks, diag_inverse, block_level, block_columns):
    rows, kk, part, bs = off_blocks.shape
    samples = right_side.shape[1]
    vmem = pl.BlockSpec(memory_space=pltpu.VMEM)
    smem = pl.BlockSpec(memory_space=pltpu.SMEM)
    anywhere = pl.BlockSpec(memory_space=pltpu.HBM)
    tile = (bs, samples)
    sent = (bs // SPLIT, samples)
    counts = [SPLIT * count for count in COUNTS]
    items = rows + 2
    dma = pltpu.SemaphoreType.DMA
    answer = pl.pallas_call(
        functools.partial(kernel, n),
        out_shape=jax.ShapeDtypeStruct((rows,) + tile, jnp.bfloat16),
        in_specs=[smem, smem, anywhere, anywhere, anywhere],
        out_specs=vmem,
        scratch_shapes=[
            pltpu.VMEM(right_side.shape, jnp.bfloat16),
            pltpu.VMEM(off_blocks.shape, jnp.bfloat16),
            pltpu.VMEM(diag_inverse.shape, jnp.bfloat16),
            pltpu.VMEM((rows,) + tile, jnp.float32),
            dma((3,)),
            pltpu.VMEM((rows - 2, 4 * part, kk * bs), jnp.bfloat16),
            pltpu.VMEM((4 * part, kk * bs), jnp.bfloat16),
            pltpu.VMEM((rows, 4 * part, bs), jnp.bfloat16),
            pltpu.VMEM((REACH * HELD + rows - FIRST[3],) + tile, jnp.bfloat16),
            pltpu.VMEM((BELOW, counts[0]) + sent, jnp.bfloat16),
            pltpu.VMEM((BELOW, counts[1]) + sent, jnp.bfloat16),
            pltpu.VMEM((BELOW, counts[2]) + sent, jnp.bfloat16),
            pltpu.VMEM((counts[0],) + sent, jnp.bfloat16),
            pltpu.VMEM((counts[1],) + sent, jnp.bfloat16),
            pltpu.VMEM((counts[2],) + sent, jnp.bfloat16),
            pltpu.VMEM((rows - FIRST[3],) + tile, jnp.bfloat16),
            pltpu.VMEM((rows, 128), jnp.int32),
            pltpu.VMEM((BELOW, rows, 128), jnp.int32),
            pltpu.SMEM((BELOW, rows, 128), jnp.int32),
            pltpu.SMEM((REACH * rows,), jnp.int32),
            pltpu.SMEM((rows,), jnp.int32),
            dma((BELOW,)), dma((BELOW,)), dma,
            dma((items,)), dma((items,)), dma((items,)), dma((items,)), dma((items,)), dma((items,)),
            dma((counts[0], 4)), dma((counts[0], BELOW)),
            dma((counts[1], 4)), dma((counts[1], BELOW)),
            dma((counts[2], 4)), dma((counts[2], BELOW)),
        ],
        compiler_params=pltpu.CompilerParams(
            collective_id=0, has_side_effects=True, vmem_limit_bytes=62 * 2 ** 20),
    )(
        block_level, block_columns, right_side, off_blocks, diag_inverse,
    )
    return jnp.swapaxes(answer, 1, 2)


def solution(mesh):
    return jax.shard_map(
        functools.partial(per_device, mesh.shape["rows"]),
        mesh=mesh,
        in_specs=(
            P("rows", "rhs", None),
            P("rows", None, "rhs", None),
            P("rows", "rhs", None),
            P("rows"),
            P("rows", None),
        ),
        out_specs=P("rows", "rhs", None),
        check_vma=False,
    )
```
